32 devices in a mesh: tm: 4 (over y, x), tile: 8 (over z, core).
Axes of the slice: x: 2, y: 2, z: 4, core: 2. Of those that a mesh axis runs over, the one named last changes fastest.
Arguments:
- first_input: bfloat16 [8, 32, 32, 384], P('tm', None, 'tile'), may hold values from -6 to 6
- second_input: bfloat16 [8, 32, 32, 384], P('tm', None, 'tile'), may hold values from -6 to 6
- output_grad: bfloat16 [8, 32, 32, 384], P('tm', None, 'tile'), may hold values from -6 to 6
- first_gain: float32 [384], replicated, may hold values from 0.1 to 1.9
- first_shift: float32 [384], replicated, may hold values from -1 to 1
- first_kernel: bfloat16 [27, 384, 384], replicated, may hold values from -1 to 1
- second_gain: float32 [384], replicated, may hold values from 0.1 to 1.9
- second_shift: float32 [384], replicated, may hold values from -1 to 1
- second_kernel: bfloat16 [27, 384, 384], replicated, may hold values from -1 to 1
- latent_kernel: bfloat16 [27, 16, 384], replicated, may hold values from -0.0625 to 0.0625
Outputs:
- latent_grad: float32 [64, 2048], P(None, ('tm', 'tile'))
The draws below stay inside these ranges and needn't reach their ends.
All inputs are finite; a program needn't handle non-finite values.
Results may differ from the reference program's by a relative error of at most 0.0044.
Values may be sent and summed in bfloat16 or wider, within the bound.
A program may use at most 64 MiB of HBM per device.

```python
import jax
import jax.numpy as jnp
from jax import lax

C = 384
L = 16
GROUPS = 32
H = 32
TT = 8
W = 32


def shared_parts(key):
    base_key = jax.random.fold_in(key, 7001)
    level_key, field_key, group_key = jax.random.split(base_key, 3)
    levels = jax.random.uniform(level_key, (W // 2,), jnp.float32, -1.0, 3.0)
    profile = jnp.repeat(levels, 2)
    raw_field = jax.random.normal(field_key, (H + 2, W + 2), jnp.float32)
    smooth = jnp.zeros((H, W), jnp.float32)
    for row_shift in range(3):
        for col_shift in range(3):
            smooth = smooth + raw_field[row_shift:row_shift + H, col_shift:col_shift + W]
    smooth = smooth / 3.0
    group_sign = jax.random.normal(group_key, (GROUPS,), jnp.float32)
    group_weight = jnp.repeat(group_sign, C // GROUPS)
    return (profile, smooth, group_weight)


def stored_draw(key, marker, profile_scale, field_scale):
    profile, smooth, group_weight = shared_parts(key)
    own_key = jax.random.fold_in(key, marker)
    noise_key, slope_key = jax.random.split(own_key, 2)
    noise_part = jax.random.normal(noise_key, (TT, H, W, C), jnp.float32)
    slopes = jax.random.normal(slope_key, (2, C), jnp.float32)
    along_profile = profile_scale * group_weight + 0.25 * slopes[0]
    along_field = field_scale * group_weight + 0.25 * slopes[1]
    result = 0.8 * noise_part + along_profile * profile[None, None, :, None] + along_field * smooth[None, :, :, None]
    return jnp.clip(result, -6.0, 6.0).astype(jnp.bfloat16)


def kernel_draw(key, marker):
    own_key = jax.random.fold_in(key, marker)
    entries = jnp.clip(jax.random.normal(own_key, (27, C, C), jnp.float32), -6.0, 6.0)
    entries = entries * (27.0 * C) ** (-0.5)
    entries = entries.at[22].add(0.5 * jnp.eye(C, dtype=jnp.float32))
    return entries.astype(jnp.bfloat16)


def draw_first_input(key, part):
    return stored_draw(key, 11, 0.5, 0.6)


def draw_second_input(key, part):
    return stored_draw(key, 12, 0.5, 0.6)


def draw_output_grad(key, part):
    return stored_draw(key, 13, 0.6, 0.6)


def draw_first_kernel(key, part):
    return kernel_draw(key, 21)


def draw_second_kernel(key, part):
    return kernel_draw(key, 22)


def noise(key, dims, spread, bound, kind=jnp.bfloat16):
    array = jax.random.normal(key, dims, jnp.float32) * spread
    return jnp.minimum(jnp.maximum(array, -bound), bound).astype(kind)


def setup_inputs(seed: int = 0) -> dict:
    arg_keys = jax.random.split(jax.random.key(seed), 11)
    first_input = draw_first_input(jax.random.fold_in(arg_keys[10], 71), 0)
    second_input = draw_second_input(jax.random.fold_in(arg_keys[10], 71), 0)
    output_grad = draw_output_grad(jax.random.fold_in(arg_keys[10], 71), 0)
    first_gain = jnp.clip(1.0 + 0.18 * jax.random.normal(arg_keys[3], (C,), jnp.float32), 0.1, 1.9)
    first_shift = jnp.clip(jax.random.uniform(arg_keys[4], (C,), jnp.float32, -1.0, 1.0), -1.0, 1.0)
    first_kernel = draw_first_kernel(jax.random.fold_in(arg_keys[10], 71), 0)
    second_gain = jnp.clip(1.0 + 0.18 * jax.random.normal(arg_keys[6], (C,), jnp.float32), 0.1, 1.9)
    second_shift = jnp.clip(jax.random.uniform(arg_keys[7], (C,), jnp.float32, -1.0, 1.0), -1.0, 1.0)
    second_kernel = draw_second_kernel(jax.random.fold_in(arg_keys[10], 71), 0)
    latent_kernel = noise(arg_keys[9], (27, L, C), (27 * C) ** -0.5, 0.0625)
    return dict(first_input=first_input, second_input=second_input, output_grad=output_grad, first_gain=first_gain, first_shift=first_shift, first_kernel=first_kernel, second_gain=second_gain, second_shift=second_shift, second_kernel=second_kernel, latent_kernel=latent_kernel)


epsilon = 1e-05

def apply_taps(padded, kernel):
    taps = kernel.reshape(3, 3, 3, kernel.shape[1], kernel.shape[2])[::-1, ::-1, ::-1]
    result = lax.conv_general_dilated(padded[None], taps, (1, 1, 1), 'VALID', dimension_numbers=('NDHWC', 'DHWOI', 'NDHWC'), preferred_element_type=jnp.float32)
    return result[0]

def backward_section(stored, grad, kernel, gain, shift):
    frame_count, row_count, col_count, channel_count = stored.shape
    values = stored.astype(jnp.float32).reshape(frame_count, row_count, col_count, GROUPS, -1)
    cell_count = row_count * col_count * values.shape[-1]
    average = lax.optimization_barrier(jnp.sum(values, axis=(1, 2, 4))) / cell_count
    variance = lax.optimization_barrier(jnp.sum(values * values, axis=(1, 2, 4))) / cell_count - average * average
    inv_std = lax.rsqrt(variance + epsilon)[:, None, None, :, None]
    normed = (values - average[:, None, None, :, None]) * inv_std
    group_gain = gain.reshape(GROUPS, -1)
    preact = normed * group_gain + shift.reshape(GROUPS, -1)
    padded = jnp.pad(grad, ((0, 2), (1, 1), (1, 1), (0, 0)))
    upstream = apply_taps(padded, kernel).reshape(values.shape)
    sigmoid_z = jax.nn.sigmoid(preact)
    through = upstream * sigmoid_z * (1.0 + preact * (1.0 - sigmoid_z)) * group_gain
    mean_grad = lax.optimization_barrier(jnp.sum(through, axis=(1, 2, 4))) / cell_count
    mean_cross = lax.optimization_barrier(jnp.sum(through * normed, axis=(1, 2, 4))) / cell_count
    result = grad.astype(jnp.float32).reshape(values.shape) + inv_std * (through - mean_grad[:, None, None, :, None] - normed * mean_cross[:, None, None, :, None])
    return result.reshape(frame_count, row_count, col_count, channel_count).astype(jnp.bfloat16)

def reference(first_input, second_input, output_grad, first_gain, first_shift, first_kernel, second_gain, second_shift, second_kernel, latent_kernel):
    second_grad = backward_section(second_input, output_grad, second_kernel, second_gain, second_shift)
    first_grad = backward_section(first_input, second_grad, first_kernel, first_gain, first_shift)
    frame_count, row_count, col_count, channel_count = first_grad.shape
    padded = jnp.pad(first_grad, ((0, 2), (1, 1), (1, 1), (0, 0)))
    pixel_grad = apply_taps(padded, latent_kernel)
    latent_count = pixel_grad.shape[-1]
    tiled = pixel_grad.reshape(frame_count, row_count // 2, 2, col_count // 2, 2, latent_count)
    tiled = jnp.transpose(tiled, (5, 2, 4, 0, 1, 3))
    return tiled.reshape(4 * latent_count, -1)
```

```python
import functools

import jax
import jax.numpy as jnp
import ml_dtypes
import numpy as np
from jax import lax
from jax.experimental import pallas as pl
from jax.experimental.pallas import tpu as pltpu
from jax.sharding import PartitionSpec as P

GROUPS = 32
MESH = pl.DeviceIdType.MESH
epsilon = 1e-05
NT = (((1,), (1,)), ((), ()))


def split3(value):
    hi = value.astype(jnp.bfloat16).astype(jnp.float32)
    rest = value - hi
    mid = rest.astype(jnp.bfloat16).astype(jnp.float32)
    return hi, mid, rest - mid


def times_exact(value, ones):
    rows = value.shape[0]
    parts = jnp.concatenate(split3(value), axis=0).astype(jnp.bfloat16)
    out = jnp.dot(parts, ones, preferred_element_type=jnp.float32)
    return out[:rows] + out[rows : 2 * rows] + out[2 * rows :]


def body(
    n_tm, n,
    x2_ref, x1_ref, g_ref, gain2, shift2, gain1, shift1, lat_ref,
    k2_hbm, k1_hbm, group_hbm, place_hbm,
    out_ref,
    g1, g2, g3, kb2, kb1, group_m, place_m, acc, xhat_s, coef_s, q_s,
    mom, sums2, sums1, outgoing, incoming,
    k_sem, c_sem, halo_send, halo_recv, st_send, st_recv, a_send, a_recv,
):
    tm = lax.axis_index("tm")
    me = lax.axis_index("tile")
    frames, cols, rows, chans = x2_ref.shape
    lat = lat_ref.shape[1]
    spot = cols * rows
    area = frames * spot
    cells = float(rows * cols * n * (chans // GROUPS))
    has_l, has_r = me > 0, me < n - 1
    has_p, has_f = tm > 0, tm < n_tm - 1
    f32 = jnp.float32

    def load(src, dst, which, a, c):
        return pltpu.make_async_copy(
            src.at[pl.ds(3 * a, 3), c],
            dst.at[pl.ds(3 * a, 3), :, pl.ds(c * chans, chans)],
            k_sem.at[which, a, c],
        )

    const_loads = [
        pltpu.make_async_copy(group_hbm, group_m, c_sem.at[0]),
        pltpu.make_async_copy(place_hbm, place_m, c_sem.at[1]),
    ]
    const_loads[0].start()
    for a in (2, 1, 0):
        for c in range(3):
            load(k2_hbm, kb2, 0, a, c).start()
    for a in (2, 1, 0):
        for c in range(3):
            load(k1_hbm, kb1, 1, a, c).start()
    const_loads[1].start()

    for buf in (g1, g2, g3):
        @pl.when(jnp.logical_not(has_l))
        def _():
            buf[:, 0] = jnp.zeros((frames + 2, rows, chans), jnp.bfloat16)

        @pl.when(jnp.logical_not(has_r))
        def _():
            buf[:, cols + 1] = jnp.zeros((frames + 2, rows, chans), jnp.bfloat16)

        @pl.when(jnp.logical_not(has_f))
        def _():
            buf[pl.ds(frames, 2)] = jnp.zeros((2, cols + 2, rows, chans), jnp.bfloat16)

    barrier = pltpu.get_barrier_semaphore()
    for d in range(1, n):
        pl.semaphore_signal(
            barrier, inc=1, device_id={"tm": tm, "tile": lax.rem(me + d, n)}, device_id_type=MESH
        )
    for dt, ok_t in ((-1, has_p), (1, has_f)):
        for dw, ok_w in ((0, None), (-1, has_l), (1, has_r)):
            ok = ok_t if ok_w is None else jnp.logical_and(ok_t, ok_w)

            @pl.when(ok)
            def _():
                pl.semaphore_signal(
                    barrier, inc=1, device_id={"tm": tm + dt, "tile": me + dw}, device_id_type=MESH
                )

    def as_int(flag):
        return jnp.where(flag, 1, 0).astype(jnp.int32)

    peers = (n - 1) + (as_int(has_p) + as_int(has_f)) * (1 + as_int(has_l) + as_int(has_r))

    g1[pl.ds(0, frames), pl.ds(1, cols)] = g_ref[...]
    stats = []
    for x_ref in (x2_ref, x1_ref):
        for f in range(frames):
            x = x_ref[f].reshape(spot, chans).astype(f32)
            stats.append(jnp.sum(x, axis=0, keepdims=True))
            stats.append(jnp.sum(x * x, axis=0, keepdims=True))
    for i, row in enumerate(stats):
        mom[me, pl.ds(i, 1)] = row
    pl.semaphore_wait(barrier, peers)

    def halo(buf, stage):
        def copy(src, dst, slot, dt, dw):
            return pltpu.make_async_remote_copy(
                src_ref=src, dst_ref=dst,
                send_sem=halo_send.at[stage, slot], recv_sem=halo_recv.at[stage, slot],
                device_id={"tm": tm + dt, "tile": me + dw}, device_id_type=MESH,
            )

        own = pl.ds(0, frames)
        both = jnp.logical_and
        side = [
            (copy(buf.at[own, cols], buf.at[own, 0], 0, 0, 1), has_r, has_l),
            (copy(buf.at[own, 1], buf.at[own, cols + 1], 1, 0, -1), has_l, has_r),
        ]
        later = []
        for f in range(2):
            at = 2 + 3 * f
            mid = pl.ds(1, cols)
            later.append([
                (copy(buf.at[f, mid], buf.at[frames + f, mid], at, -1, 0), has_p, has_f),
                (copy(buf.at[f, cols], buf.at[frames + f, 0], at + 1, -1, 1),
                 both(has_p, has_r), both(has_f, has_l)),
                (copy(buf.at[f, 1], buf.at[frames + f, cols + 1], at + 2, -1, -1),
                 both(has_p, has_l), both(has_f, has_r)),
            ])
        return side, later

    def start(moves):
        for move, sends, _ in moves:
            pl.when(sends)(move.start)

    def arrive(moves):
        for move, _, receives in moves:
            pl.when(receives)(move.wait_recv)

    def sent(moves):
        for move, sends, _ in moves:
            pl.when(sends)(move.wait_send)

    def spread(buf, sends, recvs, index, source=None):
        out = []
        for d in range(1, n):
            to = lax.rem(me + d, n)
            src = buf.at[me] if source is None else source.at[to]
            out.append((
                pltpu.make_async_remote_copy(
                    src_ref=src, dst_ref=buf.at[me],
                    send_sem=sends.at[index, d], recv_sem=recvs.at[index, d],
                    device_id={"tm": tm, "tile": to}, device_id_type=MESH,
                ),
                pltpu.make_async_remote_copy(
                    src_ref=src, dst_ref=buf.at[lax.rem(me - d + n, n)],
                    send_sem=sends.at[index, d], recv_sem=recvs.at[index, d],
                    device_id={"tm": tm, "tile": to}, device_id_type=MESH,
                ),
            ))
        return out

    def total(buf):
        out = buf[0]
        for s in range(1, n):
            out = out + buf[s]
        return out

    halos = [halo(buf, i) for i, buf in enumerate((g1, g2, g3))]
    side, later = halos[0]
    mom_moves = spread(mom, st_send, st_recv, 0)
    start(side)
    for move, _ in mom_moves:
        move.start()
    start(later[0])
    start(later[1])

    row_of = lax.broadcasted_iota(jnp.int32, (cols, rows, chans), 1).reshape(spot, chans)
    not_last, not_first = row_of < rows - 1, row_of > 0

    def conv(buf, kb, k_hbm, which, halo_parts):
        side, later = halo_parts
        for step, a in enumerate((2, 1, 0)):
            arrive(side if step == 0 else later[step - 1])
            for c in range(3):
                load(k_hbm, kb, which, a, c).wait()

            def one(b, carry):
                left = jnp.concatenate(
                    [buf[2 - a : 2 - a + frames, 2 - c : 2 - c + cols].reshape(area, chans) for c in range(3)],
                    axis=1,
                )
                part = lax.dot_general(left, kb[3 * a + b], NT, preferred_element_type=f32)
                if step == 0:
                    acc[b] = part
                else:
                    acc[b] = acc[b] + part
                return carry

            lax.fori_loop(0, 3, one, 0)

    def section(x_ref, k, tot, gain, shift, buf, nxt, kb, k_hbm, halo_parts, sums, index, next_halo):
        inv = []
        for f in range(frames):
            at = 2 * frames * k + 2 * f
            mean = tot[at : at + 1] / cells
            var = tot[at + 1 : at + 2] / cells - mean * mean
            r = lax.rsqrt(var + epsilon)
            inv.append(r)
            xhat = (x_ref[f].reshape(spot, chans).astype(f32) - mean) * r
            z = xhat * gain[...] + shift[...]
            sig = jax.nn.sigmoid(z)
            xhat_s[f] = xhat
            coef_s[f] = sig * (1.0 + z * (1.0 - sig)) * gain[...]
        conv(buf, kb, k_hbm, k, halo_parts)
        for f in range(frames):
            at = pl.ds(f * spot, spot)
            up = jnp.where(not_last, pltpu.roll(acc[0, at], spot - 1, 0), 0.0)
            down = jnp.where(not_first, pltpu.roll(acc[2, at], 1, 0), 0.0)
            q = (up + acc[1, at] + down) * coef_s[f]
            q_s[f] = q
            sums[me, pl.ds(2 * f, 1)] = jnp.sum(q, axis=0, keepdims=True)
            sums[me, pl.ds(2 * f + 1, 1)] = jnp.sum(q * xhat_s[f], axis=0, keepdims=True)
        moves = spread(sums, st_send, st_recv, index)
        for move, _ in moves:
            move.start()
        for _, move in moves:
            move.wait_recv()
        means = times_exact(total(sums), group_m[...]) / cells
        for f in range(frames):
            m1, m2 = means[2 * f : 2 * f + 1], means[2 * f + 1 : 2 * f + 2]
            own = buf[f, 1 : 1 + cols].reshape(spot, chans).astype(f32)
            dx = own + inv[f] * (q_s[f] - m1 - xhat_s[f] * m2)
            nxt[f, 1 : 1 + cols] = dx.astype(jnp.bfloat16).reshape(cols, rows, chans)
            if f == 0:
                start(next_halo[1][0])
        start(next_halo[0])
        start(next_halo[1][1])
        return moves

    for _, move in mom_moves:
        move.wait_recv()
    const_loads[0].wait()
    tot = times_exact(total(mom), group_m[...])
    moves2 = section(x2_ref, 0, tot, gain2, shift2, g1, g2, kb2, k2_hbm, halos[0], sums2, 1, halos[1])
    moves1 = section(x1_ref, 1, tot, gain1, shift1, g2, g3, kb1, k1_hbm, halos[1], sums1, 2, halos[2])

    side, later = halos[2]
    result = None
    for step, a in enumerate((2, 1, 0)):
        arrive(side if step == 0 else later[step - 1])
        weights = jnp.concatenate(
            [jnp.concatenate([lat_ref[9 * a + 3 * b + c] for c in range(3)], axis=1) for b in range(3)],
            axis=0,
        )
        pixels = jnp.concatenate(
            [g3[2 - a : 2 - a + frames, 2 - c : 2 - c + cols].reshape(area, chans) for c in range(3)],
            axis=1,
        )
        part = lax.dot_general(weights, pixels, NT, preferred_element_type=f32)
        result = part if result is None else result + part
    lane = lax.broadcasted_iota(jnp.int32, (lat, area), 1)
    lane_row = lax.rem(lane, rows)
    up = jnp.where(lane_row < rows - 1, pltpu.roll(result[:lat], area - 1, 1), 0.0)
    down = jnp.where(lane_row > 0, pltpu.roll(result[2 * lat :], 1, 1), 0.0)
    pixel = up + result[lat : 2 * lat] + down
    const_loads[1].wait()
    placed = times_exact(pixel, place_m[...])
    for j in range(n):
        outgoing[j] = placed[:, j * area : (j + 1) * area]
    last = spread(incoming, a_send, a_recv, 0, outgoing)
    for move, _ in last:
        move.start()
    incoming[me] = outgoing[me]
    for _, move in last:
        move.wait_recv()
    answer = incoming[0]
    for s in range(1, n):
        answer = answer + pltpu.roll(incoming[s], s * (cols // 2), 1)
    out_ref[...] = answer

    for side, later in halos:
        sent(side)
        sent(later[0])
        sent(later[1])
    for moves in (mom_moves, moves2, moves1, last):
        for move, _ in moves:
            move.wait_send()


def shards(
    n_tm, n,
    first_input, second_input, output_grad,
    first_gain, first_shift, first_kernel,
    second_gain, second_shift, second_kernel,
    latent_kernel,
):
    frames, rows, cols, chans = first_input.shape
    lat = latent_kernel.shape[1]
    area = frames * rows * cols
    group_of = np.arange(chans) // (chans // GROUPS)
    group = (group_of[:, None] == group_of[None]).astype(ml_dtypes.bfloat16)
    per = frames * (rows // 2) // n
    tokens = area // 4
    f, w, h = np.meshgrid(np.arange(frames), np.arange(cols), np.arange(rows), indexing="ij")
    line = f * (rows // 2) + h // 2
    target = (line // per) * area + (2 * (h % 2) + w % 2) * tokens + (line % per) * (n * cols // 2) + w // 2
    place = (target.reshape(-1, 1) == np.arange(n * area)[None]).astype(ml_dtypes.bfloat16)

    def turned(value):
        return jnp.transpose(value, (0, 2, 1, 3))

    bf16, f32 = jnp.bfloat16, jnp.float32
    vmem = pl.BlockSpec(memory_space=pltpu.VMEM)
    anywhere = pl.BlockSpec(memory_space=pl.ANY)
    grid_buf = pltpu.VMEM((frames + 2, cols + 2, rows, chans), bf16)
    kernel_buf = pltpu.VMEM((9, chans, 3 * chans), bf16)
    plane = pltpu.VMEM((frames, cols * rows, chans), f32)
    stat = -(-4 * frames // 8) * 8
    dma = pltpu.SemaphoreType.DMA
    out = pl.pallas_call(
        functools.partial(body, n_tm, n),
        out_shape=jax.ShapeDtypeStruct((lat, area), f32),
        in_specs=[vmem] * 8 + [anywhere] * 4,
        out_specs=vmem,
        scratch_shapes=[
            grid_buf, grid_buf, grid_buf, kernel_buf, kernel_buf,
            pltpu.VMEM((chans, chans), bf16),
            pltpu.VMEM((area, n * area), bf16),
            pltpu.VMEM((3, area, chans), f32),
            plane, plane, plane,
            pltpu.VMEM((n, stat, chans), f32),
            pltpu.VMEM((n, 2 * frames, chans), f32),
            pltpu.VMEM((n, 2 * frames, chans), f32),
            pltpu.VMEM((n, lat, area), f32),
            pltpu.VMEM((n, lat, area), f32),
            dma((2, 3, 3)), dma((2,)), dma((3, 8)), dma((3, 8)),
            dma((3, n)), dma((3, n)), dma((1, n)), dma((1, n)),
        ],
        compiler_params=pltpu.CompilerParams(
            collective_id=0, has_side_effects=True, vmem_limit_bytes=56 * 1024 * 1024
        ),
        cost_estimate=pl.CostEstimate(
            flops=4 * area * 27 * chans * chans, bytes_accessed=4 * 27 * chans * chans, transcendentals=2 * area * chans
        ),
    )(
        turned(second_input), turned(first_input), turned(output_grad),
        second_gain.reshape(1, -1), second_shift.reshape(1, -1),
        first_gain.reshape(1, -1), first_shift.reshape(1, -1),
        latent_kernel,
        second_kernel.reshape(9, 3, chans, chans), first_kernel.reshape(9, 3, chans, chans),
        jnp.asarray(group), jnp.asarray(place),
    )
    return out.reshape(4 * lat, tokens)


def solution(mesh):
    cells = P("tm", None, "tile", None)
    return jax.shard_map(
        functools.partial(shards, mesh.shape["tm"], mesh.shape["tile"]),
        mesh=mesh,
        in_specs=(cells,) * 3 + (P(),) * 7,
        out_specs=P(None, ("tm", "tile")),
        check_vma=False,
    )
```

```python
import functools

import jax
import jax.numpy as jnp
import ml_dtypes
import numpy as np
from jax import lax
from jax.experimental import pallas as pl
from jax.experimental.pallas import tpu as pltpu
from jax.sharding import PartitionSpec as P

GROUPS = 32
MESH = pl.DeviceIdType.MESH
epsilon = 1e-05
NT = (((1,), (1,)), ((), ()))


def split3(value):
    hi = value.astype(jnp.bfloat16).astype(jnp.float32)
    rest = value - hi
    mid = rest.astype(jnp.bfloat16).astype(jnp.float32)
    return hi, mid, rest - mid


def times_exact(value, ones):
    rows = value.shape[0]
    parts = jnp.concatenate(split3(value), axis=0).astype(jnp.bfloat16)
    out = jnp.dot(parts, ones, preferred_element_type=jnp.float32)
    return out[:rows] + out[rows : 2 * rows] + out[2 * rows :]


def body(
    n_tm, n,
    gain2, shift2, gain1, shift1, lat_ref,
    g_hbm, x2_hbm, x1_hbm, k2_hbm, k1_hbm, group_hbm, place_hbm,
    out_ref,
    raw, x_s, g1, g2, g3, kb2, kb1, group_m, place_m, acc, xhat_s, coef_s, q_s,
    mom, sums2, sums1, outgoing, incoming,
    k_sem, c_sem, halo_send, halo_recv, st_send, st_recv, a_send, a_recv,
):
    tm = lax.axis_index("tm")
    me = lax.axis_index("tile")
    frames, rows, cols, chans = g_hbm.shape
    lat = lat_ref.shape[1]
    spot = cols * rows
    area = frames * spot
    cells = float(rows * cols * n * (chans // GROUPS))
    has_l, has_r = me > 0, me < n - 1
    has_p, has_f = tm > 0, tm < n_tm - 1
    f32 = jnp.float32

    def load(src, dst, which, a, c):
        return pltpu.make_async_copy(
            src.at[pl.ds(3 * a, 3), c],
            dst.at[pl.ds(3 * a, 3), :, pl.ds(c * chans, chans)],
            k_sem.at[which, a, c],
        )

    const_loads = [
        pltpu.make_async_copy(group_hbm, group_m, c_sem.at[0]),
        pltpu.make_async_copy(place_hbm, place_m, c_sem.at[1]),
    ]
    inputs = [
        pltpu.make_async_copy(src, raw.at[i], c_sem.at[2 + i])
        for i, src in enumerate((g_hbm, x2_hbm, x1_hbm))
    ]
    for copy in inputs:
        copy.start()
    const_loads[0].start()
    for a in (2, 1, 0):
        for c in range(3):
            load(k2_hbm, kb2, 0, a, c).start()
    for a in (2, 1, 0):
        for c in range(3):
            load(k1_hbm, kb1, 1, a, c).start()
    const_loads[1].start()

    for buf in (g1, g2, g3):
        @pl.when(jnp.logical_not(has_l))
        def _():
            buf[:, 0] = jnp.zeros((frames + 2, rows, chans), jnp.bfloat16)

        @pl.when(jnp.logical_not(has_r))
        def _():
            buf[:, cols + 1] = jnp.zeros((frames + 2, rows, chans), jnp.bfloat16)

        @pl.when(jnp.logical_not(has_f))
        def _():
            buf[pl.ds(frames, 2)] = jnp.zeros((2, cols + 2, rows, chans), jnp.bfloat16)

    barrier = pltpu.get_barrier_semaphore()
    for d in range(1, n):
        pl.semaphore_signal(
            barrier, inc=1, device_id={"tm": tm, "tile": lax.rem(me + d, n)}, device_id_type=MESH
        )
    for dt, ok_t in ((-1, has_p), (1, has_f)):
        for dw, ok_w in ((0, None), (-1, has_l), (1, has_r)):
            ok = ok_t if ok_w is None else jnp.logical_and(ok_t, ok_w)

            @pl.when(ok)
            def _():
                pl.semaphore_signal(
                    barrier, inc=1, device_id={"tm": tm + dt, "tile": me + dw}, device_id_type=MESH
                )

    def as_int(flag):
        return jnp.where(flag, 1, 0).astype(jnp.int32)

    peers = (n - 1) + (as_int(has_p) + as_int(has_f)) * (1 + as_int(has_l) + as_int(has_r))

    to_w = lax.broadcasted_iota(jnp.int32, (cols, rows, spot), 0)
    to_h = lax.broadcasted_iota(jnp.int32, (cols, rows, spot), 1)
    source = lax.broadcasted_iota(jnp.int32, (cols, rows, spot), 2)
    turn = jnp.where(source == to_h * cols + to_w, 1.0, 0.0).reshape(spot, spot).astype(jnp.bfloat16)

    def turned(i, f):
        return jnp.dot(turn, raw[i, f].reshape(spot, chans), preferred_element_type=f32)

    inputs[0].wait()
    for f in range(frames):
        g1[f, 1 : 1 + cols] = turned(0, f).astype(jnp.bfloat16).reshape(cols, rows, chans)
    pl.semaphore_wait(barrier, peers)

    def halo(buf, stage):
        def copy(src, dst, slot, dt, dw):
            return pltpu.make_async_remote_copy(
                src_ref=src, dst_ref=dst,
                send_sem=halo_send.at[stage, slot], recv_sem=halo_recv.at[stage, slot],
                device_id={"tm": tm + dt, "tile": me + dw}, device_id_type=MESH,
            )

        own = pl.ds(0, frames)
        both = jnp.logical_and
        side = [
            (copy(buf.at[own, cols], buf.at[own, 0], 0, 0, 1), has_r, has_l),
            (copy(buf.at[own, 1], buf.at[own, cols + 1], 1, 0, -1), has_l, has_r),
        ]
        later = []
        for f in range(2):
            at = 2 + 3 * f
            mid = pl.ds(1, cols)
            later.append([
                (copy(buf.at[f, mid], buf.at[frames + f, mid], at, -1, 0), has_p, has_f),
                (copy(buf.at[f, cols], buf.at[frames + f, 0], at + 1, -1, 1),
                 both(has_p, has_r), both(has_f, has_l)),
                (copy(buf.at[f, 1], buf.at[frames + f, cols + 1], at + 2, -1, -1),
                 both(has_p, has_l), both(has_f, has_r)),
            ])
        return side, later

    def start(moves):
        for move, sends, _ in moves:
            pl.when(sends)(move.start)

    def arrive(moves):
        for move, _, receives in moves:
            pl.when(receives)(move.wait_recv)

    def sent(moves):
        for move, sends, _ in moves:
            pl.when(sends)(move.wait_send)

    def spread(buf, sends, recvs, index, source=None):
        out = []
        for d in range(1, n):
            to = lax.rem(me + d, n)
            src = buf.at[me] if source is None else source.at[to]
            out.append((
                pltpu.make_async_remote_copy(
                    src_ref=src, dst_ref=buf.at[me],
                    send_sem=sends.at[index, d], recv_sem=recvs.at[index, d],
                    device_id={"tm": tm, "tile": to}, device_id_type=MESH,
                ),
                pltpu.make_async_remote_copy(
                    src_ref=src, dst_ref=buf.at[lax.rem(me - d + n, n)],
                    send_sem=sends.at[index, d], recv_sem=recvs.at[index, d],
                    device_id={"tm": tm, "tile": to}, device_id_type=MESH,
                ),
            ))
        return out

    def total(buf):
        out = buf[0]
        for s in range(1, n):
            out = out + buf[s]
        return out

    halos = [halo(buf, i) for i, buf in enumerate((g1, g2, g3))]
    side, later = halos[0]
    start(side)
    start(later[0])
    start(later[1])

    for k in range(2):
        inputs[1 + k].wait()
        for f in range(frames):
            x = turned(1 + k, f)
            x_s[k, f] = x
            at = 2 * frames * k + 2 * f
            mom[me, pl.ds(at, 1)] = jnp.sum(x, axis=0, keepdims=True)
            mom[me, pl.ds(at + 1, 1)] = jnp.sum(x * x, axis=0, keepdims=True)
    mom_moves = spread(mom, st_send, st_recv, 0)
    for move, _ in mom_moves:
        move.start()

    lane_h = lax.rem(lax.broadcasted_iota(jnp.int32, (chans, spot), 1), rows)
    not_last, not_first = lane_h < rows - 1, lane_h > 0

    def conv(buf, kb, k_hbm, which, halo_parts):
        side, later = halo_parts
        for step, a in enumerate((2, 1, 0)):
            arrive(side if step == 0 else later[step - 1])
            for c in range(3):
                load(k_hbm, kb, which, a, c).wait()

            pixels = jnp.concatenate(
                [buf[2 - a : 2 - a + frames, 2 - c : 2 - c + cols].reshape(area, chans) for c in range(3)],
                axis=1,
            )
            weights = kb[3 * a : 3 * a + 3].reshape(3 * chans, 3 * chans)
            part = lax.dot_general(weights, pixels, NT, preferred_element_type=f32)
            acc[...] = part if step == 0 else acc[...] + part

    def section(k, tot, gain, shift, buf, nxt, kb, k_hbm, halo_parts, sums, index, next_halo):
        inv = []
        for f in range(frames):
            at = 2 * frames * k + 2 * f
            mean = tot[at : at + 1] / cells
            var = tot[at + 1 : at + 2] / cells - mean * mean
            r = lax.rsqrt(var + epsilon)
            inv.append(r)
            xhat = (x_s[k, f] - mean) * r
            z = xhat * gain + shift
            sig = jax.nn.sigmoid(z)
            xhat_s[f] = xhat
            coef_s[f] = sig * (1.0 + z * (1.0 - sig)) * gain
        conv(buf, kb, k_hbm, k, halo_parts)
        for f in range(frames):
            at = pl.ds(f * spot, spot)
            up = jnp.where(not_last, pltpu.roll(acc[:chans, at], spot - 1, 1), 0.0)
            down = jnp.where(not_first, pltpu.roll(acc[2 * chans :, at], 1, 1), 0.0)
            q = (up + acc[chans : 2 * chans, at] + down).T * coef_s[f]
            q_s[f] = q
            sums[me, pl.ds(2 * f, 1)] = jnp.sum(q, axis=0, keepdims=True)
            sums[me, pl.ds(2 * f + 1, 1)] = jnp.sum(q * xhat_s[f], axis=0, keepdims=True)
        moves = spread(sums, st_send, st_recv, index)
        for move, _ in moves:
            move.start()
        for _, move in moves:
            move.wait_recv()
        means = times_exact(total(sums), group_m[...]) / cells
        for f in range(frames):
            m1, m2 = means[2 * f : 2 * f + 1], means[2 * f + 1 : 2 * f + 2]
            own = buf[f, 1 : 1 + cols].reshape(spot, chans).astype(f32)
            dx = own + inv[f] * (q_s[f] - m1 - xhat_s[f] * m2)
            nxt[f, 1 : 1 + cols] = dx.astype(jnp.bfloat16).reshape(cols, rows, chans)
            if f == 0:
                start(next_halo[1][0])
        start(next_halo[0])
        start(next_halo[1][1])
        return moves

    for _, move in mom_moves:
        move.wait_recv()
    const_loads[0].wait()
    tot = times_exact(total(mom), group_m[...])

    def as_row(ref):
        return ref[...].reshape(1, chans)

    moves2 = section(0, tot, as_row(gain2), as_row(shift2), g1, g2, kb2, k2_hbm, halos[0], sums2, 1, halos[1])
    moves1 = section(1, tot, as_row(gain1), as_row(shift1), g2, g3, kb1, k1_hbm, halos[1], sums1, 2, halos[2])

    side, later = halos[2]
    result = None
    for step, a in enumerate((2, 1, 0)):
        arrive(side if step == 0 else later[step - 1])
        weights = jnp.concatenate(
            [jnp.concatenate([lat_ref[9 * a + 3 * b + c] for c in range(3)], axis=1) for b in range(3)],
            axis=0,
        )
        pixels = jnp.concatenate(
            [g3[2 - a : 2 - a + frames, 2 - c : 2 - c + cols].reshape(area, chans) for c in range(3)],
            axis=1,
        )
        part = lax.dot_general(weights, pixels, NT, preferred_element_type=f32)
        result = part if result is None else result + part
    lane = lax.broadcasted_iota(jnp.int32, (lat, area), 1)
    lane_row = lax.rem(lane, rows)
    up = jnp.where(lane_row < rows - 1, pltpu.roll(result[:lat], area - 1, 1), 0.0)
    down = jnp.where(lane_row > 0, pltpu.roll(result[2 * lat :], 1, 1), 0.0)
    pixel = up + result[lat : 2 * lat] + down
    const_loads[1].wait()
    placed = times_exact(pixel, place_m[...])
    for j in range(n):
        outgoing[j] = placed[:, j * area : (j + 1) * area]
    last = spread(incoming, a_send, a_recv, 0, outgoing)
    for move, _ in last:
        move.start()
    incoming[me] = outgoing[me]
    for _, move in last:
        move.wait_recv()
    answer = incoming[0]
    for s in range(1, n):
        answer = answer + pltpu.roll(incoming[s], s * (cols // 2), 1)
    out_ref[...] = answer

    for side, later in halos:
        sent(side)
        sent(later[0])
        sent(later[1])
    for moves in (mom_moves, moves2, moves1, last):
        for move, _ in moves:
            move.wait_send()


def shards(
    n_tm, n,
    first_input, second_input, output_grad,
    first_gain, first_shift, first_kernel,
    second_gain, second_shift, second_kernel,
    latent_kernel,
):
    frames, rows, cols, chans = first_input.shape
    lat = latent_kernel.shape[1]
    area = frames * rows * cols
    group_of = np.arange(chans) // (chans // GROUPS)
    group = (group_of[:, None] == group_of[None]).astype(ml_dtypes.bfloat16)
    per = frames * (rows // 2) // n
    tokens = area // 4
    f, w, h = np.meshgrid(np.arange(frames), np.arange(cols), np.arange(rows), indexing="ij")
    line = f * (rows // 2) + h // 2
    target = (line // per) * area + (2 * (h % 2) + w % 2) * tokens + (line % per) * (n * cols // 2) + w // 2
    place = (target.reshape(-1, 1) == np.arange(n * area)[None]).astype(ml_dtypes.bfloat16)

    bf16, f32 = jnp.bfloat16, jnp.float32
    vmem = pl.BlockSpec(memory_space=pltpu.VMEM)
    anywhere = pl.BlockSpec(memory_space=pl.ANY)
    grid_buf = pltpu.VMEM((frames + 2, cols + 2, rows, chans), bf16)
    kernel_buf = pltpu.VMEM((9, chans, 3 * chans), bf16)
    plane = pltpu.VMEM((frames, cols * rows, chans), f32)
    stat = -(-4 * frames // 8) * 8
    dma = pltpu.SemaphoreType.DMA
    out = pl.pallas_call(
        functools.partial(body, n_tm, n),
        out_shape=jax.ShapeDtypeStruct((lat, area), f32),
        in_specs=[vmem] * 5 + [anywhere] * 7,
        out_specs=vmem,
        scratch_shapes=[
            pltpu.VMEM((3, frames, rows, cols, chans), bf16),
            pltpu.VMEM((2, frames, rows * cols, chans), f32),
            grid_buf, grid_buf, grid_buf, kernel_buf, kernel_buf,
            pltpu.VMEM((chans, chans), bf16),
            pltpu.VMEM((area, n * area), bf16),
            pltpu.VMEM((3 * chans, area), f32),
            plane, plane, plane,
            pltpu.VMEM((n, stat, chans), f32),
            pltpu.VMEM((n, 2 * frames, chans), f32),
            pltpu.VMEM((n, 2 * frames, chans), f32),
            pltpu.VMEM((n, lat, area), f32),
            pltpu.VMEM((n, lat, area), f32),
            dma((2, 3, 3)), dma((5,)), dma((3, 8)), dma((3, 8)),
            dma((3, n)), dma((3, n)), dma((1, n)), dma((1, n)),
        ],
        compiler_params=pltpu.CompilerParams(
            collective_id=0, has_side_effects=True, vmem_limit_bytes=56 * 1024 * 1024
        ),
        cost_estimate=pl.CostEstimate(
            flops=4 * area * 27 * chans * chans, bytes_accessed=4 * 27 * chans * chans, transcendentals=2 * area * chans
        ),
    )(
        second_gain, second_shift, first_gain, first_shift, latent_kernel,
        output_grad, second_input, first_input,
        second_kernel.reshape(9, 3, chans, chans), first_kernel.reshape(9, 3, chans, chans),
        jnp.asarray(group), jnp.asarray(place),
    )
    return out.reshape(4 * lat, tokens)


def solution(mesh):
    cells = P("tm", None, "tile", None)
    return jax.shard_map(
        functools.partial(shards, mesh.shape["tm"], mesh.shape["tile"]),
        mesh=mesh,
        in_specs=(cells,) * 3 + (P(),) * 7,
        out_specs=P(None, ("tm", "tile")),
        check_vma=False,
    )
```

```python
import functools

import jax
import jax.numpy as jnp
import ml_dtypes
import numpy as np
from jax import lax
from jax.experimental import pallas as pl
from jax.experimental.pallas import tpu as pltpu
from jax.sharding import PartitionSpec as P

GROUPS = 32
MESH = pl.DeviceIdType.MESH
epsilon = 1e-05
NT = (((1,), (1,)), ((), ()))


def split3(value):
    hi = value.astype(jnp.bfloat16).astype(jnp.float32)
    rest = value - hi
    mid = rest.astype(jnp.bfloat16).astype(jnp.float32)
    return hi, mid, rest - mid


def times_exact(value, ones):
    rows = value.shape[0]
    parts = jnp.concatenate(split3(value), axis=0).astype(jnp.bfloat16)
    out = jnp.dot(parts, ones, preferred_element_type=jnp.float32)
    return out[:rows] + out[rows : 2 * rows] + out[2 * rows :]


def body(
    n_tm, n,
    gain2, shift2, gain1, shift1, lat_ref,
    g_hbm, x2_hbm, x1_hbm, k2_hbm, k1_hbm, group_hbm, place_hbm,
    out_ref,
    raw, x_s, g1, g2, g3, kb2, kb1, group_m, place_m, acc, xhat_s, coef_s, q_s,
    mom, mom_all, sums2, sums1, outgoing, incoming,
    k_sem, c_sem, halo_send, halo_recv, st_send, st_recv, a_send, a_recv,
):
    tm = lax.axis_index("tm")
    me = lax.axis_index("tile")
    frames, rows, cols, chans = g_hbm.shape
    lat = lat_ref.shape[1]
    spot = cols * rows
    area = frames * spot
    cells = float(rows * cols * n * (chans // GROUPS))
    has_l, has_r = me > 0, me < n - 1
    has_p, has_f = tm > 0, tm < n_tm - 1
    f32 = jnp.float32

    def load(src, dst, which, a, c):
        return pltpu.make_async_copy(
            src.at[pl.ds(3 * a, 3), c],
            dst.at[pl.ds(3 * a, 3), :, pl.ds(c * chans, chans)],
            k_sem.at[which, a, c],
        )

    const_loads = [
        pltpu.make_async_copy(group_hbm, group_m, c_sem.at[0]),
        pltpu.make_async_copy(place_hbm, place_m, c_sem.at[1]),
    ]
    inputs = [
        pltpu.make_async_copy(src, raw.at[i], c_sem.at[2 + i])
        for i, src in enumerate((g_hbm, x2_hbm, x1_hbm))
    ]
    for copy in inputs:
        copy.start()
    const_loads[0].start()
    for a in (2, 1, 0):
        for c in range(3):
            load(k2_hbm, kb2, 0, a, c).start()
    for a in (2, 1, 0):
        for c in range(3):
            load(k1_hbm, kb1, 1, a, c).start()
    const_loads[1].start()

    for buf in (g1, g2, g3):
        @pl.when(jnp.logical_not(has_l))
        def _():
            buf[:, 0] = jnp.zeros((frames + 2, rows, chans), jnp.bfloat16)

        @pl.when(jnp.logical_not(has_r))
        def _():
            buf[:, cols + 1] = jnp.zeros((frames + 2, rows, chans), jnp.bfloat16)

        @pl.when(jnp.logical_not(has_f))
        def _():
            buf[pl.ds(frames, 2)] = jnp.zeros((2, cols + 2, rows, chans), jnp.bfloat16)

    barrier = pltpu.get_barrier_semaphore()
    for d in range(1, n):
        pl.semaphore_signal(
            barrier, inc=1, device_id={"tm": tm, "tile": lax.rem(me + d, n)}, device_id_type=MESH
        )
    for dt, ok in ((-1, has_p), (1, has_f)):
        @pl.when(ok)
        def _():
            pl.semaphore_signal(
                barrier, inc=1, device_id={"tm": tm + dt, "tile": me}, device_id_type=MESH
            )

    def as_int(flag):
        return jnp.where(flag, 1, 0).astype(jnp.int32)

    peers = (n - 1) + as_int(has_p) + as_int(has_f)

    to_w = lax.broadcasted_iota(jnp.int32, (cols, rows, spot), 0)
    to_h = lax.broadcasted_iota(jnp.int32, (cols, rows, spot), 1)
    source = lax.broadcasted_iota(jnp.int32, (cols, rows, spot), 2)
    turn = jnp.where(source == to_h * cols + to_w, 1.0, 0.0).reshape(spot, spot).astype(jnp.bfloat16)

    def turned(i, f):
        return jnp.dot(turn, raw[i, f].reshape(spot, chans), preferred_element_type=f32)

    inputs[0].wait()
    for f in range(frames):
        g1[f, 1 : 1 + cols] = turned(0, f).astype(jnp.bfloat16).reshape(cols, rows, chans)
    for k in range(2):
        inputs[1 + k].wait()
        for f in range(frames):
            x = turned(1 + k, f)
            x_s[k, f] = x
            at = 2 * frames * k + 2 * f
            mom[me, pl.ds(at, 1)] = jnp.sum(x, axis=0, keepdims=True)
            mom[me, pl.ds(at + 1, 1)] = jnp.sum(x * x, axis=0, keepdims=True)
    pl.semaphore_wait(barrier, peers)

    def halo(buf, stage):
        def copy(src, dst, slot, dt, dw):
            return pltpu.make_async_remote_copy(
                src_ref=src, dst_ref=dst,
                send_sem=halo_send.at[stage, slot], recv_sem=halo_recv.at[stage, slot],
                device_id={"tm": tm + dt, "tile": me + dw}, device_id_type=MESH,
            )

        own, next_two, first_two = pl.ds(0, frames), pl.ds(frames, 2), pl.ds(0, 2)
        inner = pl.ds(2, cols - 2)
        both = jnp.logical_and
        side = [
            (copy(buf.at[own, cols], buf.at[own, 0], 0, 0, 1), has_r, has_l),
            (copy(buf.at[own, 1], buf.at[own, cols + 1], 1, 0, -1), has_l, has_r),
        ]
        edges = [
            (copy(buf.at[first_two, col], buf.at[next_two, col], slot, -1, 0), has_p, has_f)
            for slot, col in ((2, 1), (3, cols))
        ]
        inners = [
            [(copy(buf.at[f, inner], buf.at[frames + f, inner], 4 + f, -1, 0), has_p, has_f)]
            for f in range(2)
        ]
        passed = [
            (copy(buf.at[next_two, cols], buf.at[next_two, 0], 6, 0, 1),
             both(has_f, has_r), both(has_f, has_l)),
            (copy(buf.at[next_two, 1], buf.at[next_two, cols + 1], 7, 0, -1),
             both(has_f, has_l), both(has_f, has_r)),
        ]
        return side, edges, inners, passed

    def start(moves):
        for move, sends, _ in moves:
            pl.when(sends)(move.start)

    def arrive(moves):
        for move, _, receives in moves:
            pl.when(receives)(move.wait_recv)

    def sent(moves):
        for move, sends, _ in moves:
            pl.when(sends)(move.wait_send)

    def spread(buf, sends, recvs, index, source=None):
        out = []
        for d in range(1, n):
            to = lax.rem(me + d, n)
            src = buf.at[me] if source is None else source.at[to]
            out.append((
                pltpu.make_async_remote_copy(
                    src_ref=src, dst_ref=buf.at[me],
                    send_sem=sends.at[index, d], recv_sem=recvs.at[index, d],
                    device_id={"tm": tm, "tile": to}, device_id_type=MESH,
                ),
                pltpu.make_async_remote_copy(
                    src_ref=src, dst_ref=buf.at[lax.rem(me - d + n, n)],
                    send_sem=sends.at[index, d], recv_sem=recvs.at[index, d],
                    device_id={"tm": tm, "tile": to}, device_id_type=MESH,
                ),
            ))
        return out

    def total(buf):
        out = buf[0]
        for s in range(1, n):
            out = out + buf[s]
        return out

    halos = [halo(buf, i) for i, buf in enumerate((g1, g2, g3))]
    def send_own(moves):
        start(moves[0])
        start(moves[1])
        for part in moves[2]:
            start(part)

    mom_moves = spread(mom, st_send, st_recv, 0)
    start(halos[0][0])
    for move, _ in mom_moves:
        move.start()
    start(halos[0][1])
    for part in halos[0][2]:
        start(part)

    lane_h = lax.rem(lax.broadcasted_iota(jnp.int32, (chans, spot), 1), rows)
    not_last, not_first = lane_h < rows - 1, lane_h > 0

    def frames_ready(moves, step):
        side, edges, inners, passed = moves
        if step == 0:
            arrive(side)
        elif step == 1:
            arrive(inners[0])
            arrive(passed)
        else:
            arrive(inners[1])

    def pass_on(moves):
        arrive(moves[1])
        start(moves[3])

    def conv(buf, kb, k_hbm, which, moves, between):
        for step, a in enumerate((2, 1, 0)):
            frames_ready(moves, step)
            for c in range(3):
                load(k_hbm, kb, which, a, c).wait()
            pixels = jnp.concatenate(
                [buf[2 - a : 2 - a + frames, 2 - c : 2 - c + cols].reshape(area, chans) for c in range(3)],
                axis=1,
            )
            weights = kb[3 * a : 3 * a + 3].reshape(3 * chans, 3 * chans)
            part = lax.dot_general(weights, pixels, NT, preferred_element_type=f32)
            acc[...] = part if step == 0 else acc[...] + part
            if step == 0:
                pass_on(moves)
                between()

    def section(k, gain, shift, buf, nxt, kb, k_hbm, moves, sums, index, next_moves):
        inv = []

        def factors():
            if k == 0:
                for _, move in mom_moves:
                    move.wait_recv()
                const_loads[0].wait()
                mom_all[...] = times_exact(total(mom), group_m[...])
            for f in range(frames):
                at = 2 * frames * k + 2 * f
                mean = mom_all[at : at + 1] / cells
                var = mom_all[at + 1 : at + 2] / cells - mean * mean
                r = lax.rsqrt(var + epsilon)
                inv.append(r)
                xhat = (x_s[k, f] - mean) * r
                z = xhat * gain + shift
                sig = jax.nn.sigmoid(z)
                xhat_s[f] = xhat
                coef_s[f] = sig * (1.0 + z * (1.0 - sig)) * gain

        conv(buf, kb, k_hbm, k, moves, factors)
        for f in range(frames):
            at = pl.ds(f * spot, spot)
            up = jnp.where(not_last, pltpu.roll(acc[:chans, at], spot - 1, 1), 0.0)
            down = jnp.where(not_first, pltpu.roll(acc[2 * chans :, at], 1, 1), 0.0)
            q = (up + acc[chans : 2 * chans, at] + down).T * coef_s[f]
            q_s[f] = q
            sums[me, pl.ds(2 * f, 1)] = jnp.sum(q, axis=0, keepdims=True)
            sums[me, pl.ds(2 * f + 1, 1)] = jnp.sum(q * xhat_s[f], axis=0, keepdims=True)
        sum_moves = spread(sums, st_send, st_recv, index)
        for move, _ in sum_moves:
            move.start()
        for _, move in sum_moves:
            move.wait_recv()
        means = times_exact(total(sums), group_m[...]) / cells
        for f in range(frames):
            m1, m2 = means[2 * f : 2 * f + 1], means[2 * f + 1 : 2 * f + 2]
            own = buf[f, 1 : 1 + cols].reshape(spot, chans).astype(f32)
            dx = own + inv[f] * (q_s[f] - m1 - xhat_s[f] * m2)
            nxt[f, 1 : 1 + cols] = dx.astype(jnp.bfloat16).reshape(cols, rows, chans)
        send_own(next_moves)
        return sum_moves

    def as_row(ref):
        return ref[...].reshape(1, chans)

    moves2 = section(0, as_row(gain2), as_row(shift2), g1, g2, kb2, k2_hbm, halos[0], sums2, 1, halos[1])
    moves1 = section(1, as_row(gain1), as_row(shift1), g2, g3, kb1, k1_hbm, halos[1], sums1, 2, halos[2])

    result = None
    for step, a in enumerate((2, 1, 0)):
        frames_ready(halos[2], step)
        weights = jnp.concatenate(
            [jnp.concatenate([lat_ref[9 * a + 3 * b + c] for c in range(3)], axis=1) for b in range(3)],
            axis=0,
        )
        pixels = jnp.concatenate(
            [g3[2 - a : 2 - a + frames, 2 - c : 2 - c + cols].reshape(area, chans) for c in range(3)],
            axis=1,
        )
        part = lax.dot_general(weights, pixels, NT, preferred_element_type=f32)
        result = part if result is None else result + part
        if step == 0:
            pass_on(halos[2])
    lane = lax.broadcasted_iota(jnp.int32, (lat, area), 1)
    lane_row = lax.rem(lane, rows)
    up = jnp.where(lane_row < rows - 1, pltpu.roll(result[:lat], area - 1, 1), 0.0)
    down = jnp.where(lane_row > 0, pltpu.roll(result[2 * lat :], 1, 1), 0.0)
    pixel = up + result[lat : 2 * lat] + down
    const_loads[1].wait()
    placed = times_exact(pixel, place_m[...])
    for j in range(n):
        outgoing[j] = placed[:, j * area : (j + 1) * area]
    last = spread(incoming, a_send, a_recv, 0, outgoing)
    for move, _ in last:
        move.start()
    incoming[me] = outgoing[me]
    for _, move in last:
        move.wait_recv()
    answer = incoming[0]
    for s in range(1, n):
        answer = answer + pltpu.roll(incoming[s], s * (cols // 2), 1)
    out_ref[...] = answer

    for side, edges, inners, passed in halos:
        for part in (side, edges, inners[0], inners[1], passed):
            sent(part)
    for moves in (mom_moves, moves2, moves1, last):
        for move, _ in moves:
            move.wait_send()


def shards(
    n_tm, n,
    first_input, second_input, output_grad,
    first_gain, first_shift, first_kernel,
    second_gain, second_shift, second_kernel,
    latent_kernel,
):
    frames, rows, cols, chans = first_input.shape
    lat = latent_kernel.shape[1]
    area = frames * rows * cols
    group_of = np.arange(chans) // (chans // GROUPS)
    group = (group_of[:, None] == group_of[None]).astype(ml_dtypes.bfloat16)
    per = frames * (rows // 2) // n
    tokens = area // 4
    f, w, h = np.meshgrid(np.arange(frames), np.arange(cols), np.arange(rows), indexing="ij")
    line = f * (rows // 2) + h // 2
    target = (line // per) * area + (2 * (h % 2) + w % 2) * tokens + (line % per) * (n * cols // 2) + w // 2
    place = (target.reshape(-1, 1) == np.arange(n * area)[None]).astype(ml_dtypes.bfloat16)

    bf16, f32 = jnp.bfloat16, jnp.float32
    vmem = pl.BlockSpec(memory_space=pltpu.VMEM)
    anywhere = pl.BlockSpec(memory_space=pl.ANY)
    grid_buf = pltpu.VMEM((frames + 2, cols + 2, rows, chans), bf16)
    kernel_buf = pltpu.VMEM((9, chans, 3 * chans), bf16)
    plane = pltpu.VMEM((frames, cols * rows, chans), f32)
    stat = -(-4 * frames // 8) * 8
    dma = pltpu.SemaphoreType.DMA
    out = pl.pallas_call(
        functools.partial(body, n_tm, n),
        out_shape=jax.ShapeDtypeStruct((lat, area), f32),
        in_specs=[vmem] * 5 + [anywhere] * 7,
        out_specs=vmem,
        scratch_shapes=[
            pltpu.VMEM((3, frames, rows, cols, chans), bf16),
            pltpu.VMEM((2, frames, rows * cols, chans), f32),
            grid_buf, grid_buf, grid_buf, kernel_buf, kernel_buf,
            pltpu.VMEM((chans, chans), bf16),
            pltpu.VMEM((area, n * area), bf16),
            pltpu.VMEM((3 * chans, area), f32),
            plane, plane, plane,
            pltpu.VMEM((n, stat, chans), f32),
            pltpu.VMEM((stat, chans), f32),
            pltpu.VMEM((n, 2 * frames, chans), f32),
            pltpu.VMEM((n, 2 * frames, chans), f32),
            pltpu.VMEM((n, lat, area), f32),
            pltpu.VMEM((n, lat, area), f32),
            dma((2, 3, 3)), dma((5,)), dma((3, 8)), dma((3, 8)),
            dma((3, n)), dma((3, n)), dma((1, n)), dma((1, n)),
        ],
        compiler_params=pltpu.CompilerParams(
            collective_id=0, has_side_effects=True, vmem_limit_bytes=56 * 1024 * 1024
        ),
        cost_estimate=pl.CostEstimate(
            flops=4 * area * 27 * chans * chans, bytes_accessed=4 * 27 * chans * chans, transcendentals=2 * area * chans
        ),
    )(
        second_gain, second_shift, first_gain, first_shift, latent_kernel,
        output_grad, second_input, first_input,
        second_kernel.reshape(9, 3, chans, chans), first_kernel.reshape(9, 3, chans, chans),
        jnp.asarray(group), jnp.asarray(place),
    )
    return out.reshape(4 * lat, tokens)


def solution(mesh):
    cells = P("tm", None, "tile", None)
    return jax.shard_map(
        functools.partial(shards, mesh.shape["tm"], mesh.shape["tile"]),
        mesh=mesh,
        in_specs=(cells,) * 3 + (P(),) * 7,
        out_specs=P(None, ("tm", "tile")),
        check_vma=False,
    )
```

```python
import functools

import jax
import jax.numpy as jnp
import ml_dtypes
import numpy as np
from jax import lax
from jax.experimental import pallas as pl
from jax.experimental.pallas import tpu as pltpu
from jax.sharding import PartitionSpec as P

GROUPS = 32
MESH = pl.DeviceIdType.MESH
epsilon = 1e-05
NT = (((1,), (1,)), ((), ()))


def split3(value):
    hi = value.astype(jnp.bfloat16).astype(jnp.float32)
    rest = value - hi
    mid = rest.astype(jnp.bfloat16).astype(jnp.float32)
    return hi, mid, rest - mid


def times_exact(value, ones):
    rows = value.shape[0]
    parts = jnp.concatenate(split3(value), axis=0).astype(jnp.bfloat16)
    out = jnp.dot(parts, ones, preferred_element_type=jnp.float32)
    return out[:rows] + out[rows : 2 * rows] + out[2 * rows :]


def body(
    n_tm, n,
    gain2, shift2, gain1, shift1, lat_ref,
    g_hbm, x2_hbm, x1_hbm, k2_hbm, k1_hbm, group_hbm, place_hbm,
    out_ref,
    raw, x_s, g1, g2, g3, kb2, kb1, group_m, place_m, acc, xhat_s, coef_s, q_s,
    mom, mom_all, sums2, sums1, outgoing, incoming,
    k_sem, c_sem, halo_send, halo_recv, st_send, st_recv, a_send, a_recv,
):
    tm = lax.axis_index("tm")
    me = lax.axis_index("tile")
    frames, rows, cols, chans = g_hbm.shape
    lat = lat_ref.shape[1]
    spot = cols * rows
    area = frames * spot
    cells = float(rows * cols * n * (chans // GROUPS))
    has_l, has_r = me > 0, me < n - 1
    has_p, has_f = tm > 0, tm < n_tm - 1
    f32 = jnp.float32

    def load(src, dst, which, a, c):
        return pltpu.make_async_copy(
            src.at[pl.ds(3 * a, 3), c],
            dst.at[pl.ds(3 * a, 3), :, pl.ds(c * chans, chans)],
            k_sem.at[which, a, c],
        )

    const_loads = [
        pltpu.make_async_copy(group_hbm, group_m, c_sem.at[0]),
        pltpu.make_async_copy(place_hbm, place_m, c_sem.at[1]),
    ]
    inputs = [
        pltpu.make_async_copy(src, raw.at[i], c_sem.at[2 + i])
        for i, src in enumerate((g_hbm, x2_hbm, x1_hbm))
    ]
    for copy in inputs:
        copy.start()
    const_loads[0].start()
    for c in range(3):
        load(k2_hbm, kb2, 0, 2, c).start()

    for buf in (g1, g2, g3):
        @pl.when(jnp.logical_not(has_l))
        def _():
            buf[:, 0] = jnp.zeros((frames + 2, rows, chans), jnp.bfloat16)

        @pl.when(jnp.logical_not(has_r))
        def _():
            buf[:, cols + 1] = jnp.zeros((frames + 2, rows, chans), jnp.bfloat16)

        @pl.when(jnp.logical_not(has_f))
        def _():
            buf[pl.ds(frames, 2)] = jnp.zeros((2, cols + 2, rows, chans), jnp.bfloat16)

    barrier = pltpu.get_barrier_semaphore()
    for d in range(1, n):
        pl.semaphore_signal(
            barrier, inc=1, device_id={"tm": tm, "tile": lax.rem(me + d, n)}, device_id_type=MESH
        )
    for dt, ok in ((-1, has_p), (1, has_f)):
        @pl.when(ok)
        def _():
            pl.semaphore_signal(
                barrier, inc=1, device_id={"tm": tm + dt, "tile": me}, device_id_type=MESH
            )

    def as_int(flag):
        return jnp.where(flag, 1, 0).astype(jnp.int32)

    peers = (n - 1) + as_int(has_p) + as_int(has_f)

    to_w = lax.broadcasted_iota(jnp.int32, (cols, rows, spot), 0)
    to_h = lax.broadcasted_iota(jnp.int32, (cols, rows, spot), 1)
    source = lax.broadcasted_iota(jnp.int32, (cols, rows, spot), 2)
    turn = jnp.where(source == to_h * cols + to_w, 1.0, 0.0).reshape(spot, spot).astype(jnp.bfloat16)

    def turned(i, f):
        return jnp.dot(turn, raw[i, f].reshape(spot, chans), preferred_element_type=f32)

    inputs[0].wait()
    for f in range(frames):
        g1[f, 1 : 1 + cols] = turned(0, f).astype(jnp.bfloat16).reshape(cols, rows, chans)
    for k in range(2):
        inputs[1 + k].wait()
        for f in range(frames):
            x = turned(1 + k, f)
            x_s[k, f] = x
            at = 2 * frames * k + 2 * f
            mom[me, pl.ds(at, 1)] = jnp.sum(x, axis=0, keepdims=True)
            mom[me, pl.ds(at + 1, 1)] = jnp.sum(x * x, axis=0, keepdims=True)
    pl.semaphore_wait(barrier, peers)

    def halo(buf, stage):
        def copy(src, dst, slot, dt, dw):
            return pltpu.make_async_remote_copy(
                src_ref=src, dst_ref=dst,
                send_sem=halo_send.at[stage, slot], recv_sem=halo_recv.at[stage, slot],
                device_id={"tm": tm + dt, "tile": me + dw}, device_id_type=MESH,
            )

        own, next_two, first_two = pl.ds(0, frames), pl.ds(frames, 2), pl.ds(0, 2)
        inner = pl.ds(2, cols - 2)
        both = jnp.logical_and
        side = [
            (copy(buf.at[own, cols], buf.at[own, 0], 0, 0, 1), has_r, has_l),
            (copy(buf.at[own, 1], buf.at[own, cols + 1], 1, 0, -1), has_l, has_r),
        ]
        edges = [
            (copy(buf.at[first_two, col], buf.at[next_two, col], slot, -1, 0), has_p, has_f)
            for slot, col in ((2, 1), (3, cols))
        ]
        inners = [
            [(copy(buf.at[f, inner], buf.at[frames + f, inner], 4 + f, -1, 0), has_p, has_f)]
            for f in range(2)
        ]
        passed = [
            (copy(buf.at[next_two, cols], buf.at[next_two, 0], 6, 0, 1),
             both(has_f, has_r), both(has_f, has_l)),
            (copy(buf.at[next_two, 1], buf.at[next_two, cols + 1], 7, 0, -1),
             both(has_f, has_l), both(has_f, has_r)),
        ]
        return side, edges, inners, passed

    def start(moves):
        for move, sends, _ in moves:
            pl.when(sends)(move.start)

    def arrive(moves):
        for move, _, receives in moves:
            pl.when(receives)(move.wait_recv)

    def sent(moves):
        for move, sends, _ in moves:
            pl.when(sends)(move.wait_send)

    def spread(buf, sends, recvs, index, source=None):
        out = []
        for d in range(1, n):
            to = lax.rem(me + d, n)
            src = buf.at[me] if source is None else source.at[to]
            out.append((
                pltpu.make_async_remote_copy(
                    src_ref=src, dst_ref=buf.at[me],
                    send_sem=sends.at[index, d], recv_sem=recvs.at[index, d],
                    device_id={"tm": tm, "tile": to}, device_id_type=MESH,
                ),
                pltpu.make_async_remote_copy(
                    src_ref=src, dst_ref=buf.at[lax.rem(me - d + n, n)],
                    send_sem=sends.at[index, d], recv_sem=recvs.at[index, d],
                    device_id={"tm": tm, "tile": to}, device_id_type=MESH,
                ),
            ))
        return out

    def total(buf):
        out = buf[0]
        for s in range(1, n):
            out = out + buf[s]
        return out

    halos = [halo(buf, i) for i, buf in enumerate((g1, g2, g3))]
    def send_own(moves):
        start(moves[0])
        start(moves[1])
        for part in moves[2]:
            start(part)

    mom_moves = spread(mom, st_send, st_recv, 0)
    start(halos[0][0])
    for move, _ in mom_moves:
        move.start()
    start(halos[0][1])
    for part in halos[0][2]:
        start(part)
    for a in (1, 0):
        for c in range(3):
            load(k2_hbm, kb2, 0, a, c).start()

    lane_h = lax.rem(lax.broadcasted_iota(jnp.int32, (chans, spot), 1), rows)
    not_last, not_first = lane_h < rows - 1, lane_h > 0

    def frames_ready(moves, step):
        side, edges, inners, passed = moves
        if step == 0:
            arrive(side)
        elif step == 1:
            arrive(inners[0])
            arrive(passed)
        else:
            arrive(inners[1])

    def pass_on(moves):
        arrive(moves[1])
        start(moves[3])

    def conv(buf, kb, k_hbm, which, moves, between):
        for step, a in enumerate((2, 1, 0)):
            frames_ready(moves, step)
            for c in range(3):
                load(k_hbm, kb, which, a, c).wait()
            pixels = jnp.concatenate(
                [buf[2 - a : 2 - a + frames, 2 - c : 2 - c + cols].reshape(area, chans) for c in range(3)],
                axis=1,
            )
            weights = kb[3 * a : 3 * a + 3].reshape(3 * chans, 3 * chans)
            part = lax.dot_general(weights, pixels, NT, preferred_element_type=f32)
            acc[...] = part if step == 0 else acc[...] + part
            if step == 0:
                pass_on(moves)
                between()

    def section(k, gain, shift, buf, nxt, kb, k_hbm, moves, sums, index, next_moves):
        inv = []

        def factors():
            if k == 0:
                for _, move in mom_moves:
                    move.wait_recv()
                for a in (2, 1, 0):
                    for c in range(3):
                        load(k1_hbm, kb1, 1, a, c).start()
                const_loads[1].start()
                const_loads[0].wait()
                mom_all[...] = times_exact(total(mom), group_m[...])
            for f in range(frames):
                at = 2 * frames * k + 2 * f
                mean = mom_all[at : at + 1] / cells
                var = mom_all[at + 1 : at + 2] / cells - mean * mean
                r = lax.rsqrt(var + epsilon)
                inv.append(r)
                xhat = (x_s[k, f] - mean) * r
                z = xhat * gain + shift
                sig = jax.nn.sigmoid(z)
                xhat_s[f] = xhat
                coef_s[f] = sig * (1.0 + z * (1.0 - sig)) * gain

        conv(buf, kb, k_hbm, k, moves, factors)
        for f in range(frames):
            at = pl.ds(f * spot, spot)
            up = jnp.where(not_last, pltpu.roll(acc[:chans, at], spot - 1, 1), 0.0)
            down = jnp.where(not_first, pltpu.roll(acc[2 * chans :, at], 1, 1), 0.0)
            q = (up + acc[chans : 2 * chans, at] + down).T * coef_s[f]
            q_s[f] = q
            sums[me, pl.ds(2 * f, 1)] = jnp.sum(q, axis=0, keepdims=True)
            sums[me, pl.ds(2 * f + 1, 1)] = jnp.sum(q * xhat_s[f], axis=0, keepdims=True)
        sum_moves = spread(sums, st_send, st_recv, index)
        for move, _ in sum_moves:
            move.start()
        for _, move in sum_moves:
            move.wait_recv()
        means = times_exact(total(sums), group_m[...]) / cells
        for f in range(frames):
            m1, m2 = means[2 * f : 2 * f + 1], means[2 * f + 1 : 2 * f + 2]
            own = buf[f, 1 : 1 + cols].reshape(spot, chans).astype(f32)
            dx = own + inv[f] * (q_s[f] - m1 - xhat_s[f] * m2)
            nxt[f, 1 : 1 + cols] = dx.astype(jnp.bfloat16).reshape(cols, rows, chans)
        send_own(next_moves)
        return sum_moves

    def as_row(ref):
        return ref[...].reshape(1, chans)

    moves2 = section(0, as_row(gain2), as_row(shift2), g1, g2, kb2, k2_hbm, halos[0], sums2, 1, halos[1])
    moves1 = section(1, as_row(gain1), as_row(shift1), g2, g3, kb1, k1_hbm, halos[1], sums1, 2, halos[2])

    result = None
    for step, a in enumerate((2, 1, 0)):
        frames_ready(halos[2], step)
        weights = jnp.concatenate(
            [jnp.concatenate([lat_ref[9 * a + 3 * b + c] for c in range(3)], axis=1) for b in range(3)],
            axis=0,
        )
        pixels = jnp.concatenate(
            [g3[2 - a : 2 - a + frames, 2 - c : 2 - c + cols].reshape(area, chans) for c in range(3)],
            axis=1,
        )
        part = lax.dot_general(weights, pixels, NT, preferred_element_type=f32)
        result = part if result is None else result + part
        if step == 0:
            pass_on(halos[2])
    lane = lax.broadcasted_iota(jnp.int32, (lat, area), 1)
    lane_row = lax.rem(lane, rows)
    up = jnp.where(lane_row < rows - 1, pltpu.roll(result[:lat], area - 1, 1), 0.0)
    down = jnp.where(lane_row > 0, pltpu.roll(result[2 * lat :], 1, 1), 0.0)
    pixel = up + result[lat : 2 * lat] + down
    const_loads[1].wait()
    placed = times_exact(pixel, place_m[...])
    half = area // 2
    for j in range(n):
        outgoing[j] = placed[:, j * half : (j + 1) * half]
    last = spread(incoming, a_send, a_recv, 0, outgoing)
    for move, _ in last:
        move.start()
    incoming[me] = outgoing[me]
    for _, move in last:
        move.wait_recv()
    width = n * cols // 2
    low = lax.rem(lax.broadcasted_iota(jnp.int32, (lat, half), 1), width) < width // 2
    lower = upper = jnp.zeros((lat, half), f32)
    for s in range(n):
        got = incoming[s]
        lower = lower + pltpu.roll(jnp.where(low, got, 0.0), s * (cols // 2), 1)
        upper = upper + pltpu.roll(jnp.where(low, 0.0, got), (half + s * (cols // 2) - width // 2) % half, 1)
    out_ref[...] = jnp.concatenate([lower, upper], axis=1)

    for side, edges, inners, passed in halos:
        for part in (side, edges, inners[0], inners[1], passed):
            sent(part)
    for moves in (mom_moves, moves2, moves1, last):
        for move, _ in moves:
            move.wait_send()


def shards(
    n_tm, n,
    first_input, second_input, output_grad,
    first_gain, first_shift, first_kernel,
    second_gain, second_shift, second_kernel,
    latent_kernel,
):
    frames, rows, cols, chans = first_input.shape
    lat = latent_kernel.shape[1]
    area = frames * rows * cols
    group_of = np.arange(chans) // (chans // GROUPS)
    group = (group_of[:, None] == group_of[None]).astype(ml_dtypes.bfloat16)
    per = frames * (rows // 2) // n
    tokens = area // 4
    f, w, h = np.meshgrid(np.arange(frames), np.arange(cols), np.arange(rows), indexing="ij")
    line = f * (rows // 2) + h // 2
    width = n * cols // 2
    target = (line // per) * (area // 2) + (h % 2) * (width // 2) + (w % 2) * tokens + (line % per) * width + w // 2
    place = (target.reshape(-1, 1) == np.arange(n * area // 2)[None]).astype(ml_dtypes.bfloat16)

    bf16, f32 = jnp.bfloat16, jnp.float32
    vmem = pl.BlockSpec(memory_space=pltpu.VMEM)
    anywhere = pl.BlockSpec(memory_space=pl.ANY)
    grid_buf = pltpu.VMEM((frames + 2, cols + 2, rows, chans), bf16)
    kernel_buf = pltpu.VMEM((9, chans, 3 * chans), bf16)
    plane = pltpu.VMEM((frames, cols * rows, chans), f32)
    stat = -(-4 * frames // 8) * 8
    dma = pltpu.SemaphoreType.DMA
    out = pl.pallas_call(
        functools.partial(body, n_tm, n),
        out_shape=jax.ShapeDtypeStruct((lat, area), f32),
        in_specs=[vmem] * 5 + [anywhere] * 7,
        out_specs=vmem,
        scratch_shapes=[
            pltpu.VMEM((3, frames, rows, cols, chans), bf16),
            pltpu.VMEM((2, frames, rows * cols, chans), f32),
            grid_buf, grid_buf, grid_buf, kernel_buf, kernel_buf,
            pltpu.VMEM((chans, chans), bf16),
            pltpu.VMEM((area, n * area // 2), bf16),
            pltpu.VMEM((3 * chans, area), f32),
            plane, plane, plane,
            pltpu.VMEM((n, stat, chans), f32),
            pltpu.VMEM((stat, chans), f32),
            pltpu.VMEM((n, 2 * frames, chans), f32),
            pltpu.VMEM((n, 2 * frames, chans), f32),
            pltpu.VMEM((n, lat, area // 2), f32),
            pltpu.VMEM((n, lat, area // 2), f32),
            dma((2, 3, 3)), dma((5,)), dma((3, 8)), dma((3, 8)),
            dma((3, n)), dma((3, n)), dma((1, n)), dma((1, n)),
        ],
        compiler_params=pltpu.CompilerParams(
            collective_id=0, has_side_effects=True, vmem_limit_bytes=56 * 1024 * 1024
        ),
        cost_estimate=pl.CostEstimate(
            flops=4 * area * 27 * chans * chans, bytes_accessed=4 * 27 * chans * chans, transcendentals=2 * area * chans
        ),
    )(
        second_gain, second_shift, first_gain, first_shift, latent_kernel,
        output_grad, second_input, first_input,
        second_kernel.reshape(9, 3, chans, chans), first_kernel.reshape(9, 3, chans, chans),
        jnp.asarray(group), jnp.asarray(place),
    )
    return out.reshape(4 * lat, tokens)


def solution(mesh):
    cells = P("tm", None, "tile", None)
    return jax.shard_map(
        functools.partial(shards, mesh.shape["tm"], mesh.shape["tile"]),
        mesh=mesh,
        in_specs=(cells,) * 3 + (P(),) * 7,
        out_specs=P(None, ("tm", "tile")),
        check_vma=False,
    )
```

```python
import functools

import jax
import jax.numpy as jnp
import ml_dtypes
import numpy as np
from jax import lax
from jax.experimental import pallas as pl
from jax.experimental.pallas import tpu as pltpu
from jax.sharding import PartitionSpec as P

GROUPS = 32
MESH = pl.DeviceIdType.MESH
epsilon = 1e-05
NT = (((1,), (1,)), ((), ()))


def split3(value):
    hi = value.astype(jnp.bfloat16).astype(jnp.float32)
    rest = value - hi
    mid = rest.astype(jnp.bfloat16).astype(jnp.float32)
    return hi, mid, rest - mid


def times_exact(value, ones):
    rows = value.shape[0]
    parts = jnp.concatenate(split3(value), axis=0).astype(jnp.bfloat16)
    out = jnp.dot(parts, ones, preferred_element_type=jnp.float32)
    return out[:rows] + out[rows : 2 * rows] + out[2 * rows :]


def body(
    n_tm, n,
    gain2, shift2, gain1, shift1, lat_ref,
    g_hbm, x2_hbm, x1_hbm, k2_hbm, k1_hbm, group_hbm, place_hbm,
    out_ref,
    raw, x_s, g1, g2, g3, kb2, kb1, group_m, place_m, acc, xhat_s, coef_s, q_s,
    mom, mom_all, sums2, sums1, outgoing, incoming,
    k_sem, c_sem, halo_send, halo_recv, st_send, st_recv, a_send, a_recv,
):
    tm = lax.axis_index("tm")
    me = lax.axis_index("tile")
    frames, rows, cols, chans = g_hbm.shape
    lat = lat_ref.shape[1]
    spot = cols * rows
    area = frames * spot
    cells = float(rows * cols * n * (chans // GROUPS))
    has_l, has_r = me > 0, me < n - 1
    has_p, has_f = tm > 0, tm < n_tm - 1
    f32 = jnp.float32

    def load(src, dst, which, a, c):
        return pltpu.make_async_copy(
            src.at[pl.ds(3 * a, 3), c],
            dst.at[pl.ds(3 * a, 3), :, pl.ds(c * chans, chans)],
            k_sem.at[which, a, c],
        )

    const_loads = [
        pltpu.make_async_copy(group_hbm, group_m, c_sem.at[0]),
        pltpu.make_async_copy(place_hbm, place_m, c_sem.at[1]),
    ]
    inputs = [
        pltpu.make_async_copy(src, raw.at[i], c_sem.at[2 + i])
        for i, src in enumerate((g_hbm, x2_hbm, x1_hbm))
    ]
    for copy in inputs:
        copy.start()
    const_loads[0].start()
    for c in range(3):
        load(k2_hbm, kb2, 0, 2, c).start()

    for buf in (g1, g2, g3):
        @pl.when(jnp.logical_not(has_l))
        def _():
            buf[:, 0] = jnp.zeros((frames + 2, rows, chans), jnp.bfloat16)

        @pl.when(jnp.logical_not(has_r))
        def _():
            buf[:, cols + 1] = jnp.zeros((frames + 2, rows, chans), jnp.bfloat16)

        @pl.when(jnp.logical_not(has_f))
        def _():
            buf[pl.ds(frames, 2)] = jnp.zeros((2, cols + 2, rows, chans), jnp.bfloat16)

    barrier = pltpu.get_barrier_semaphore()
    for d in range(1, n):
        pl.semaphore_signal(
            barrier, inc=1, device_id={"tm": tm, "tile": lax.rem(me + d, n)}, device_id_type=MESH
        )
    for dt, ok in ((-1, has_p), (1, has_f)):
        @pl.when(ok)
        def _():
            pl.semaphore_signal(
                barrier, inc=1, device_id={"tm": tm + dt, "tile": me}, device_id_type=MESH
            )

    def as_int(flag):
        return jnp.where(flag, 1, 0).astype(jnp.int32)

    peers = (n - 1) + as_int(has_p) + as_int(has_f)

    to_w = lax.broadcasted_iota(jnp.int32, (cols, rows, spot), 0)
    to_h = lax.broadcasted_iota(jnp.int32, (cols, rows, spot), 1)
    source = lax.broadcasted_iota(jnp.int32, (cols, rows, spot), 2)
    turn = jnp.where(source == to_h * cols + to_w, 1.0, 0.0).reshape(spot, spot).astype(jnp.bfloat16)

    def turned(i, f):
        return jnp.dot(turn, raw[i, f].reshape(spot, chans), preferred_element_type=f32)

    inputs[0].wait()
    for f in range(frames):
        g1[f, 1 : 1 + cols] = turned(0, f).astype(jnp.bfloat16).reshape(cols, rows, chans)
    for k in range(2):
        inputs[1 + k].wait()
        for f in range(frames):
            x = turned(1 + k, f)
            x_s[k, f] = x
            at = 2 * frames * k + 2 * f
            mom[me, pl.ds(at, 1)] = jnp.sum(x, axis=0, keepdims=True)
            mom[me, pl.ds(at + 1, 1)] = jnp.sum(x * x, axis=0, keepdims=True)
    pl.semaphore_wait(barrier, peers)

    def halo(buf, stage):
        def copy(src, dst, slot, dt, dw):
            return pltpu.make_async_remote_copy(
                src_ref=src, dst_ref=dst,
                send_sem=halo_send.at[stage, slot], recv_sem=halo_recv.at[stage, slot],
                device_id={"tm": tm + dt, "tile": me + dw}, device_id_type=MESH,
            )

        own, next_two, first_two = pl.ds(0, frames), pl.ds(frames, 2), pl.ds(0, 2)
        inner = pl.ds(2, cols - 2)
        both = jnp.logical_and
        side = [
            (copy(buf.at[own, cols], buf.at[own, 0], 0, 0, 1), has_r, has_l),
            (copy(buf.at[own, 1], buf.at[own, cols + 1], 1, 0, -1), has_l, has_r),
        ]
        edges = [
            (copy(buf.at[first_two, col], buf.at[next_two, col], slot, -1, 0), has_p, has_f)
            for slot, col in ((2, 1), (3, cols))
        ]
        inners = [
            [(copy(buf.at[f, inner], buf.at[frames + f, inner], 4 + f, -1, 0), has_p, has_f)]
            for f in range(2)
        ]
        passed = [
            (copy(buf.at[next_two, cols], buf.at[next_two, 0], 6, 0, 1),
             both(has_f, has_r), both(has_f, has_l)),
            (copy(buf.at[next_two, 1], buf.at[next_two, cols + 1], 7, 0, -1),
             both(has_f, has_l), both(has_f, has_r)),
        ]
        return side, edges, inners, passed

    def start(moves):
        for move, sends, _ in moves:
            pl.when(sends)(move.start)

    def arrive(moves):
        for move, _, receives in moves:
            pl.when(receives)(move.wait_recv)

    def sent(moves):
        for move, sends, _ in moves:
            pl.when(sends)(move.wait_send)

    def spread(buf, sends, recvs, index, source=None):
        out = []
        for d in range(1, n):
            to = lax.rem(me + d, n)
            src = buf.at[me] if source is None else source.at[to]
            out.append((
                pltpu.make_async_remote_copy(
                    src_ref=src, dst_ref=buf.at[me],
                    send_sem=sends.at[index, d], recv_sem=recvs.at[index, d],
                    device_id={"tm": tm, "tile": to}, device_id_type=MESH,
                ),
                pltpu.make_async_remote_copy(
                    src_ref=src, dst_ref=buf.at[lax.rem(me - d + n, n)],
                    send_sem=sends.at[index, d], recv_sem=recvs.at[index, d],
                    device_id={"tm": tm, "tile": to}, device_id_type=MESH,
                ),
            ))
        return out

    def total(buf):
        out = buf[0]
        for s in range(1, n):
            out = out + buf[s]
        return out

    halos = [halo(buf, i) for i, buf in enumerate((g1, g2, g3))]
    def send_own(moves):
        start(moves[0])
        start(moves[1])
        for part in moves[2]:
            start(part)

    mom_moves = spread(mom, st_send, st_recv, 0)
    start(halos[0][0])
    for move, _ in mom_moves:
        move.start()
    start(halos[0][1])
    for part in halos[0][2]:
        start(part)
    for a in (1, 0):
        for c in range(3):
            load(k2_hbm, kb2, 0, a, c).start()

    lane_h = lax.rem(lax.broadcasted_iota(jnp.int32, (chans, spot), 1), rows)
    not_last, not_first = lane_h < rows - 1, lane_h > 0

    groups = [[(2, 1)], [(2, 0), (2, 2)], [(1, 1), (0, 1)], [(1, 0), (1, 2), (0, 0), (0, 2)]]

    def group_ready(moves, step, between=lambda: None):
        side, edges, inners, passed = moves
        if step == 1:
            arrive(side)
        elif step == 2:
            arrive(edges)
            start(passed)
            between()
            arrive(inners[0])
            arrive(inners[1])
        elif step == 3:
            arrive(passed)

    def pixels_of(buf, pairs):
        return jnp.concatenate(
            [buf[2 - a : 2 - a + frames, 2 - c : 2 - c + cols].reshape(area, chans) for a, c in pairs], axis=1
        )

    def conv(buf, kb, k_hbm, which, moves, between):
        for step, pairs in enumerate(groups):
            group_ready(moves, step, between)
            for a, c in pairs:
                load(k_hbm, kb, which, a, c).wait()
            weights = jnp.concatenate(
                [kb[3 * a : 3 * a + 3, :, c * chans : (c + 1) * chans].reshape(3 * chans, chans) for a, c in pairs],
                axis=1,
            )
            part = lax.dot_general(weights, pixels_of(buf, pairs), NT, preferred_element_type=f32)
            acc[...] = part if step == 0 else acc[...] + part

    def section(k, gain, shift, buf, nxt, kb, k_hbm, moves, sums, index, next_moves):
        inv = []

        def factors():
            if k == 0:
                for _, move in mom_moves:
                    move.wait_recv()
                for a in (2, 1, 0):
                    for c in range(3):
                        load(k1_hbm, kb1, 1, a, c).start()
                const_loads[1].start()
                const_loads[0].wait()
                mom_all[...] = times_exact(total(mom), group_m[...])
            for f in range(frames):
                at = 2 * frames * k + 2 * f
                mean = mom_all[at : at + 1] / cells
                var = mom_all[at + 1 : at + 2] / cells - mean * mean
                r = lax.rsqrt(var + epsilon)
                inv.append(r)
                xhat = (x_s[k, f] - mean) * r
                z = xhat * gain + shift
                sig = jax.nn.sigmoid(z)
                xhat_s[f] = xhat
                coef_s[f] = sig * (1.0 + z * (1.0 - sig)) * gain

        conv(buf, kb, k_hbm, k, moves, factors)
        for f in range(frames):
            at = pl.ds(f * spot, spot)
            up = jnp.where(not_last, pltpu.roll(acc[:chans, at], spot - 1, 1), 0.0)
            down = jnp.where(not_first, pltpu.roll(acc[2 * chans :, at], 1, 1), 0.0)
            q = (up + acc[chans : 2 * chans, at] + down).T * coef_s[f]
            q_s[f] = q
            sums[me, pl.ds(2 * f, 1)] = jnp.sum(q, axis=0, keepdims=True)
            sums[me, pl.ds(2 * f + 1, 1)] = jnp.sum(q * xhat_s[f], axis=0, keepdims=True)
        sum_moves = spread(sums, st_send, st_recv, index)
        for move, _ in sum_moves:
            move.start()
        for _, move in sum_moves:
            move.wait_recv()
        means = times_exact(total(sums), group_m[...]) / cells
        for f in range(frames):
            m1, m2 = means[2 * f : 2 * f + 1], means[2 * f + 1 : 2 * f + 2]
            own = buf[f, 1 : 1 + cols].reshape(spot, chans).astype(f32)
            dx = own + inv[f] * (q_s[f] - m1 - xhat_s[f] * m2)
            nxt[f, 1 : 1 + cols] = dx.astype(jnp.bfloat16).reshape(cols, rows, chans)
        send_own(next_moves)
        return sum_moves

    def as_row(ref):
        return ref[...].reshape(1, chans)

    moves2 = section(0, as_row(gain2), as_row(shift2), g1, g2, kb2, k2_hbm, halos[0], sums2, 1, halos[1])
    moves1 = section(1, as_row(gain1), as_row(shift1), g2, g3, kb1, k1_hbm, halos[1], sums1, 2, halos[2])

    result = None
    for step, pairs in enumerate(groups):
        group_ready(halos[2], step)
        weights = jnp.concatenate(
            [jnp.concatenate([lat_ref[9 * a + 3 * b + c] for a, c in pairs], axis=1) for b in range(3)], axis=0
        )
        part = lax.dot_general(weights, pixels_of(g3, pairs), NT, preferred_element_type=f32)
        result = part if result is None else result + part
    lane = lax.broadcasted_iota(jnp.int32, (lat, area), 1)
    lane_row = lax.rem(lane, rows)
    up = jnp.where(lane_row < rows - 1, pltpu.roll(result[:lat], area - 1, 1), 0.0)
    down = jnp.where(lane_row > 0, pltpu.roll(result[2 * lat :], 1, 1), 0.0)
    pixel = up + result[lat : 2 * lat] + down
    const_loads[1].wait()
    placed = times_exact(pixel, place_m[...])
    half = area // 2
    for j in range(n):
        outgoing[j] = placed[:, j * half : (j + 1) * half]
    last = spread(incoming, a_send, a_recv, 0, outgoing)
    for move, _ in last:
        move.start()
    incoming[me] = outgoing[me]
    for _, move in last:
        move.wait_recv()
    width = n * cols // 2
    low = lax.rem(lax.broadcasted_iota(jnp.int32, (lat, half), 1), width) < width // 2
    lower = upper = jnp.zeros((lat, half), f32)
    for s in range(n):
        got = incoming[s]
        lower = lower + pltpu.roll(jnp.where(low, got, 0.0), s * (cols // 2), 1)
        upper = upper + pltpu.roll(jnp.where(low, 0.0, got), (half + s * (cols // 2) - width // 2) % half, 1)
    out_ref[...] = jnp.concatenate([lower, upper], axis=1)

    for side, edges, inners, passed in halos:
        for part in (side, edges, inners[0], inners[1], passed):
            sent(part)
    for moves in (mom_moves, moves2, moves1, last):
        for move, _ in moves:
            move.wait_send()


def shards(
    n_tm, n,
    first_input, second_input, output_grad,
    first_gain, first_shift, first_kernel,
    second_gain, second_shift, second_kernel,
    latent_kernel,
):
    frames, rows, cols, chans = first_input.shape
    lat = latent_kernel.shape[1]
    area = frames * rows * cols
    group_of = np.arange(chans) // (chans // GROUPS)
    group = (group_of[:, None] == group_of[None]).astype(ml_dtypes.bfloat16)
    per = frames * (rows // 2) // n
    tokens = area // 4
    f, w, h = np.meshgrid(np.arange(frames), np.arange(cols), np.arange(rows), indexing="ij")
    line = f * (rows // 2) + h // 2
    width = n * cols // 2
    target = (line // per) * (area // 2) + (h % 2) * (width // 2) + (w % 2) * tokens + (line % per) * width + w // 2
    place = (target.reshape(-1, 1) == np.arange(n * area // 2)[None]).astype(ml_dtypes.bfloat16)

    bf16, f32 = jnp.bfloat16, jnp.float32
    vmem = pl.BlockSpec(memory_space=pltpu.VMEM)
    anywhere = pl.BlockSpec(memory_space=pl.ANY)
    grid_buf = pltpu.VMEM((frames + 2, cols + 2, rows, chans), bf16)
    kernel_buf = pltpu.VMEM((9, chans, 3 * chans), bf16)
    plane = pltpu.VMEM((frames, cols * rows, chans), f32)
    stat = -(-4 * frames // 8) * 8
    dma = pltpu.SemaphoreType.DMA
    out = pl.pallas_call(
        functools.partial(body, n_tm, n),
        out_shape=jax.ShapeDtypeStruct((lat, area), f32),
        in_specs=[vmem] * 5 + [anywhere] * 7,
        out_specs=vmem,
        scratch_shapes=[
            pltpu.VMEM((3, frames, rows, cols, chans), bf16),
            pltpu.VMEM((2, frames, rows * cols, chans), f32),
            grid_buf, grid_buf, grid_buf, kernel_buf, kernel_buf,
            pltpu.VMEM((chans, chans), bf16),
            pltpu.VMEM((area, n * area // 2), bf16),
            pltpu.VMEM((3 * chans, area), f32),
            plane, plane, plane,
            pltpu.VMEM((n, stat, chans), f32),
            pltpu.VMEM((stat, chans), f32),
            pltpu.VMEM((n, 2 * frames, chans), f32),
            pltpu.VMEM((n, 2 * frames, chans), f32),
            pltpu.VMEM((n, lat, area // 2), f32),
            pltpu.VMEM((n, lat, area // 2), f32),
            dma((2, 3, 3)), dma((5,)), dma((3, 8)), dma((3, 8)),
            dma((3, n)), dma((3, n)), dma((1, n)), dma((1, n)),
        ],
        compiler_params=pltpu.CompilerParams(
            collective_id=0, has_side_effects=True, vmem_limit_bytes=56 * 1024 * 1024
        ),
        cost_estimate=pl.CostEstimate(
            flops=4 * area * 27 * chans * chans, bytes_accessed=4 * 27 * chans * chans, transcendentals=2 * area * chans
        ),
    )(
        second_gain, second_shift, first_gain, first_shift, latent_kernel,
        output_grad, second_input, first_input,
        second_kernel.reshape(9, 3, chans, chans), first_kernel.reshape(9, 3, chans, chans),
        jnp.asarray(group), jnp.asarray(place),
    )
    return out.reshape(4 * lat, tokens)


def solution(mesh):
    cells = P("tm", None, "tile", None)
    return jax.shard_map(
        functools.partial(shards, mesh.shape["tm"], mesh.shape["tile"]),
        mesh=mesh,
        in_specs=(cells,) * 3 + (P(),) * 7,
        out_specs=P(None, ("tm", "tile")),
        check_vma=False,
    )
```

```python
import functools

import jax
import jax.numpy as jnp
import ml_dtypes
import numpy as np
from jax import lax
from jax.experimental import pallas as pl
from jax.experimental.pallas import tpu as pltpu
from jax.sharding import PartitionSpec as P

GROUPS = 32
MESH = pl.DeviceIdType.MESH
epsilon = 1e-05
NT = (((1,), (1,)), ((), ()))


def split3(value):
    hi = value.astype(jnp.bfloat16).astype(jnp.float32)
    rest = value - hi
    mid = rest.astype(jnp.bfloat16).astype(jnp.float32)
    return hi, mid, rest - mid


def times_exact(value, ones):
    rows = value.shape[0]
    parts = jnp.concatenate(split3(value), axis=0).astype(jnp.bfloat16)
    out = jnp.dot(parts, ones, preferred_element_type=jnp.float32)
    return out[:rows] + out[rows : 2 * rows] + out[2 * rows :]


def body(
    n_tm, n,
    gain2, shift2, gain1, shift1, lat_ref,
    g_hbm, x2_hbm, x1_hbm, k2_hbm, k1_hbm, group_hbm, place_hbm,
    out_ref,
    raw, x_s, x_b, x_e, q_e, g1, g2, g3, kb2, kb1, group_m, place_m, acc, xhat_s, coef_s, q_s,
    mom, mom_all, sums2, sums1, outgoing, incoming,
    k_sem, c_sem, halo_send, halo_recv, e_send, e_recv, st_send, st_recv, a_send, a_recv,
):
    tm = lax.axis_index("tm")
    me = lax.axis_index("tile")
    frames, rows, cols, chans = g_hbm.shape
    lat = lat_ref.shape[1]
    spot = cols * rows
    area = frames * spot
    cells = float(rows * cols * n * (chans // GROUPS))
    has_l, has_r = me > 0, me < n - 1
    has_p, has_f = tm > 0, tm < n_tm - 1
    f32 = jnp.float32

    def load(src, dst, which, a, c):
        return pltpu.make_async_copy(
            src.at[pl.ds(3 * a, 3), c],
            dst.at[pl.ds(3 * a, 3), :, pl.ds(c * chans, chans)],
            k_sem.at[which, a, c],
        )

    const_loads = [
        pltpu.make_async_copy(group_hbm, group_m, c_sem.at[0]),
        pltpu.make_async_copy(place_hbm, place_m, c_sem.at[1]),
    ]
    inputs = [
        pltpu.make_async_copy(src, raw.at[i], c_sem.at[2 + i])
        for i, src in enumerate((g_hbm, x2_hbm, x1_hbm))
    ]
    for copy in inputs:
        copy.start()
    const_loads[0].start()
    for c in range(3):
        load(k2_hbm, kb2, 0, 2, c).start()

    for buf in (g1, g2, g3):
        @pl.when(jnp.logical_not(has_l))
        def _():
            buf[:, 0] = jnp.zeros((frames + 2, rows, chans), jnp.bfloat16)

        @pl.when(jnp.logical_not(has_r))
        def _():
            buf[:, cols + 1] = jnp.zeros((frames + 2, rows, chans), jnp.bfloat16)

        @pl.when(jnp.logical_not(has_f))
        def _():
            buf[pl.ds(frames, 2)] = jnp.zeros((2, cols + 2, rows, chans), jnp.bfloat16)

    barrier = pltpu.get_barrier_semaphore()
    for d in range(1, n):
        pl.semaphore_signal(
            barrier, inc=1, device_id={"tm": tm, "tile": lax.rem(me + d, n)}, device_id_type=MESH
        )
    for dt, ok in ((-1, has_p), (1, has_f)):
        @pl.when(ok)
        def _():
            pl.semaphore_signal(
                barrier, inc=1, device_id={"tm": tm + dt, "tile": me}, device_id_type=MESH
            )

    def as_int(flag):
        return jnp.where(flag, 1, 0).astype(jnp.int32)

    peers = (n - 1) + as_int(has_p) + as_int(has_f)

    to_w = lax.broadcasted_iota(jnp.int32, (cols, rows, spot), 0)
    to_h = lax.broadcasted_iota(jnp.int32, (cols, rows, spot), 1)
    source = lax.broadcasted_iota(jnp.int32, (cols, rows, spot), 2)
    turn = jnp.where(source == to_h * cols + to_w, 1.0, 0.0).reshape(spot, spot).astype(jnp.bfloat16)

    def turned(i, f):
        return jnp.dot(turn, raw[i, f].reshape(spot, chans), preferred_element_type=f32)

    inputs[0].wait()
    for f in range(frames):
        g1[f, 1 : 1 + cols] = turned(0, f).astype(jnp.bfloat16).reshape(cols, rows, chans)
    for k in range(2):
        inputs[1 + k].wait()
        for f in range(frames):
            x = turned(1 + k, f)
            x_s[k, f] = x
            x_b[k, f] = x.astype(jnp.bfloat16).reshape(cols, rows, chans)
            at = 2 * frames * k + 2 * f
            mom[me, pl.ds(at, 1)] = jnp.sum(x, axis=0, keepdims=True)
            mom[me, pl.ds(at + 1, 1)] = jnp.sum(x * x, axis=0, keepdims=True)
    pl.semaphore_wait(barrier, peers)

    def halo(buf, stage):
        def copy(src, dst, slot, dt, dw):
            return pltpu.make_async_remote_copy(
                src_ref=src, dst_ref=dst,
                send_sem=halo_send.at[stage, slot], recv_sem=halo_recv.at[stage, slot],
                device_id={"tm": tm + dt, "tile": me + dw}, device_id_type=MESH,
            )

        own, next_two, first_two = pl.ds(0, frames), pl.ds(frames, 2), pl.ds(0, 2)
        inner = pl.ds(2, cols - 2)
        both = jnp.logical_and
        side = [
            (copy(buf.at[own, cols], buf.at[own, 0], 0, 0, 1), has_r, has_l),
            (copy(buf.at[own, 1], buf.at[own, cols + 1], 1, 0, -1), has_l, has_r),
        ]
        edges = [
            (copy(buf.at[first_two, col], buf.at[next_two, col], slot, -1, 0), has_p, has_f)
            for slot, col in ((2, 1), (3, cols))
        ]
        inners = [
            [(copy(buf.at[f, inner], buf.at[frames + f, inner], 4 + f, -1, 0), has_p, has_f)]
            for f in range(2)
        ]
        passed = [
            (copy(buf.at[next_two, cols], buf.at[next_two, 0], 6, 0, 1),
             both(has_f, has_r), both(has_f, has_l)),
            (copy(buf.at[next_two, 1], buf.at[next_two, cols + 1], 7, 0, -1),
             both(has_f, has_l), both(has_f, has_r)),
        ]
        return (side if stage == 0 else []), edges, inners, passed

    def edge_moves(src_last, src_first, dst, at):
        def copy(src, to, slot, dw):
            return pltpu.make_async_remote_copy(
                src_ref=src, dst_ref=to, send_sem=e_send.at[slot], recv_sem=e_recv.at[slot],
                device_id={"tm": tm, "tile": me + dw}, device_id_type=MESH,
            )

        return [
            (copy(src_last, dst.at[0], at, 1), has_r, has_l),
            (copy(src_first, dst.at[1], at + 1, -1), has_l, has_r),
        ]

    every = pl.ds(0, frames)
    x_edges = [
        edge_moves(x_b.at[k, every, cols - 1], x_b.at[k, every, 0], x_e.at[k], 2 * k) for k in range(2)
    ]
    q_edges = [
        edge_moves(
            q_s.at[k, every, pl.ds(spot - rows, rows)], q_s.at[k, every, pl.ds(0, rows)], q_e.at[k], 4 + 2 * k
        )
        for k in range(2)
    ]

    def start(moves):
        for move, sends, _ in moves:
            pl.when(sends)(move.start)

    def arrive(moves):
        for move, _, receives in moves:
            pl.when(receives)(move.wait_recv)

    def sent(moves):
        for move, sends, _ in moves:
            pl.when(sends)(move.wait_send)

    def spread(buf, sends, recvs, index, source=None):
        out = []
        for d in range(1, n):
            to = lax.rem(me + d, n)
            src = buf.at[me] if source is None else source.at[to]
            out.append((
                pltpu.make_async_remote_copy(
                    src_ref=src, dst_ref=buf.at[me],
                    send_sem=sends.at[index, d], recv_sem=recvs.at[index, d],
                    device_id={"tm": tm, "tile": to}, device_id_type=MESH,
                ),
                pltpu.make_async_remote_copy(
                    src_ref=src, dst_ref=buf.at[lax.rem(me - d + n, n)],
                    send_sem=sends.at[index, d], recv_sem=recvs.at[index, d],
                    device_id={"tm": tm, "tile": to}, device_id_type=MESH,
                ),
            ))
        return out

    def total(buf):
        out = buf[0]
        for s in range(1, n):
            out = out + buf[s]
        return out

    halos = [halo(buf, i) for i, buf in enumerate((g1, g2, g3))]
    def send_own(moves):
        start(moves[0])
        start(moves[1])
        for part in moves[2]:
            start(part)

    mom_moves = spread(mom, st_send, st_recv, 0)
    start(halos[0][0])
    for move, _ in mom_moves:
        move.start()
    start(halos[0][1])
    for part in halos[0][2]:
        start(part)
    for a in (1, 0):
        for c in range(3):
            load(k2_hbm, kb2, 0, a, c).start()
    for k in range(2):
        start(x_edges[k])

    lane_h = lax.rem(lax.broadcasted_iota(jnp.int32, (chans, spot), 1), rows)
    not_last, not_first = lane_h < rows - 1, lane_h > 0

    groups = [[(2, 1)], [(2, 0), (2, 2)], [(1, 1), (0, 1)], [(1, 0), (1, 2), (0, 0), (0, 2)]]

    def group_ready(moves, step, between=lambda: None):
        side, edges, inners, passed = moves
        if step == 1:
            arrive(side)
        elif step == 2:
            arrive(edges)
            start(passed)
            between()
            arrive(inners[0])
            arrive(inners[1])
        elif step == 3:
            arrive(passed)

    def pixels_of(buf, pairs):
        return jnp.concatenate(
            [buf[2 - a : 2 - a + frames, 2 - c : 2 - c + cols].reshape(area, chans) for a, c in pairs], axis=1
        )

    def conv(buf, kb, k_hbm, which, moves, between):
        for step, pairs in enumerate(groups):
            group_ready(moves, step, between)
            for a, c in pairs:
                load(k_hbm, kb, which, a, c).wait()
            weights = jnp.concatenate(
                [kb[3 * a : 3 * a + 3, :, c * chans : (c + 1) * chans].reshape(3 * chans, chans) for a, c in pairs],
                axis=1,
            )
            part = lax.dot_general(weights, pixels_of(buf, pairs), NT, preferred_element_type=f32)
            acc[...] = part if step == 0 else acc[...] + part

    def section(k, gain, shift, buf, nxt, kb, k_hbm, moves, sums, index, next_moves):
        inv, averages = [], []

        def factors():
            if k == 0:
                for _, move in mom_moves:
                    move.wait_recv()
                for a in (2, 1, 0):
                    for c in range(3):
                        load(k1_hbm, kb1, 1, a, c).start()
                const_loads[1].start()
                const_loads[0].wait()
                mom_all[...] = times_exact(total(mom), group_m[...])
            for f in range(frames):
                at = 2 * frames * k + 2 * f
                mean = mom_all[at : at + 1] / cells
                var = mom_all[at + 1 : at + 2] / cells - mean * mean
                r = lax.rsqrt(var + epsilon)
                inv.append(r)
                averages.append(mean)
                xhat = (x_s[k, f] - mean) * r
                z = xhat * gain + shift
                sig = jax.nn.sigmoid(z)
                xhat_s[f] = xhat
                coef_s[f] = sig * (1.0 + z * (1.0 - sig)) * gain

        conv(buf, kb, k_hbm, k, moves, factors)
        for f in range(frames):
            at = pl.ds(f * spot, spot)
            up = jnp.where(not_last, pltpu.roll(acc[:chans, at], spot - 1, 1), 0.0)
            down = jnp.where(not_first, pltpu.roll(acc[2 * chans :, at], 1, 1), 0.0)
            q = (up + acc[chans : 2 * chans, at] + down).T * coef_s[f]
            q_s[k, f] = q
            sums[me, pl.ds(2 * f, 1)] = jnp.sum(q, axis=0, keepdims=True)
            sums[me, pl.ds(2 * f + 1, 1)] = jnp.sum(q * xhat_s[f], axis=0, keepdims=True)
        sum_moves = spread(sums, st_send, st_recv, index)
        for move, _ in sum_moves:
            move.start()
        start(q_edges[k])
        for _, move in sum_moves:
            move.wait_recv()
        means = times_exact(total(sums), group_m[...]) / cells
        for f in range(frames):
            m1, m2 = means[2 * f : 2 * f + 1], means[2 * f + 1 : 2 * f + 2]
            own = buf[f, 1 : 1 + cols].reshape(spot, chans).astype(f32)
            dx = own + inv[f] * (q_s[k, f] - m1 - xhat_s[f] * m2)
            nxt[f, 1 : 1 + cols] = dx.astype(jnp.bfloat16).reshape(cols, rows, chans)
        send_own(next_moves)
        arrive(x_edges[k])
        arrive(q_edges[k])
        for at, (col, there) in enumerate(((0, has_l), (cols + 1, has_r))):
            @pl.when(there)
            def _():
                for f in range(frames):
                    m1, m2 = means[2 * f : 2 * f + 1], means[2 * f + 1 : 2 * f + 2]
                    xhat = (x_e[k, at, f].astype(f32) - averages[f]) * inv[f]
                    dx = buf[f, col].astype(f32) + inv[f] * (q_e[k, at, f] - m1 - xhat * m2)
                    nxt[f, col] = dx.astype(jnp.bfloat16)
        return sum_moves

    def as_row(ref):
        return ref[...].reshape(1, chans)

    moves2 = section(0, as_row(gain2), as_row(shift2), g1, g2, kb2, k2_hbm, halos[0], sums2, 1, halos[1])
    moves1 = section(1, as_row(gain1), as_row(shift1), g2, g3, kb1, k1_hbm, halos[1], sums1, 2, halos[2])

    result = None
    for step, pairs in enumerate(groups):
        group_ready(halos[2], step)
        weights = jnp.concatenate(
            [jnp.concatenate([lat_ref[9 * a + 3 * b + c] for a, c in pairs], axis=1) for b in range(3)], axis=0
        )
        part = lax.dot_general(weights, pixels_of(g3, pairs), NT, preferred_element_type=f32)
        result = part if result is None else result + part
    lane = lax.broadcasted_iota(jnp.int32, (lat, area), 1)
    lane_row = lax.rem(lane, rows)
    up = jnp.where(lane_row < rows - 1, pltpu.roll(result[:lat], area - 1, 1), 0.0)
    down = jnp.where(lane_row > 0, pltpu.roll(result[2 * lat :], 1, 1), 0.0)
    pixel = up + result[lat : 2 * lat] + down
    const_loads[1].wait()
    placed = times_exact(pixel, place_m[...])
    half = area // 2
    for j in range(n):
        outgoing[j] = placed[:, j * half : (j + 1) * half]
    last = spread(incoming, a_send, a_recv, 0, outgoing)
    for move, _ in last:
        move.start()
    incoming[me] = outgoing[me]
    for _, move in last:
        move.wait_recv()
    width = n * cols // 2
    low = lax.rem(lax.broadcasted_iota(jnp.int32, (lat, half), 1), width) < width // 2
    lower = upper = jnp.zeros((lat, half), f32)
    for s in range(n):
        got = incoming[s]
        lower = lower + pltpu.roll(jnp.where(low, got, 0.0), s * (cols // 2), 1)
        upper = upper + pltpu.roll(jnp.where(low, 0.0, got), (half + s * (cols // 2) - width // 2) % half, 1)
    out_ref[...] = jnp.concatenate([lower, upper], axis=1)

    for side, edges, inners, passed in halos:
        for part in (side, edges, inners[0], inners[1], passed):
            sent(part)
    for moves in (*x_edges, *q_edges):
        sent(moves)
    for moves in (mom_moves, moves2, moves1, last):
        for move, _ in moves:
            move.wait_send()


def shards(
    n_tm, n,
    first_input, second_input, output_grad,
    first_gain, first_shift, first_kernel,
    second_gain, second_shift, second_kernel,
    latent_kernel,
):
    frames, rows, cols, chans = first_input.shape
    lat = latent_kernel.shape[1]
    area = frames * rows * cols
    group_of = np.arange(chans) // (chans // GROUPS)
    group = (group_of[:, None] == group_of[None]).astype(ml_dtypes.bfloat16)
    per = frames * (rows // 2) // n
    tokens = area // 4
    f, w, h = np.meshgrid(np.arange(frames), np.arange(cols), np.arange(rows), indexing="ij")
    line = f * (rows // 2) + h // 2
    width = n * cols // 2
    target = (line // per) * (area // 2) + (h % 2) * (width // 2) + (w % 2) * tokens + (line % per) * width + w // 2
    place = (target.reshape(-1, 1) == np.arange(n * area // 2)[None]).astype(ml_dtypes.bfloat16)

    bf16, f32 = jnp.bfloat16, jnp.float32
    vmem = pl.BlockSpec(memory_space=pltpu.VMEM)
    anywhere = pl.BlockSpec(memory_space=pl.ANY)
    grid_buf = pltpu.VMEM((frames + 2, cols + 2, rows, chans), bf16)
    kernel_buf = pltpu.VMEM((9, chans, 3 * chans), bf16)
    plane = pltpu.VMEM((frames, cols * rows, chans), f32)
    stat = -(-4 * frames // 8) * 8
    dma = pltpu.SemaphoreType.DMA
    out = pl.pallas_call(
        functools.partial(body, n_tm, n),
        out_shape=jax.ShapeDtypeStruct((lat, area), f32),
        in_specs=[vmem] * 5 + [anywhere] * 7,
        out_specs=vmem,
        scratch_shapes=[
            pltpu.VMEM((3, frames, rows, cols, chans), bf16),
            pltpu.VMEM((2, frames, rows * cols, chans), f32),
            pltpu.VMEM((2, frames, cols, rows, chans), bf16),
            pltpu.VMEM((2, 2, frames, rows, chans), bf16),
            pltpu.VMEM((2, 2, frames, rows, chans), f32),
            grid_buf, grid_buf, grid_buf, kernel_buf, kernel_buf,
            pltpu.VMEM((chans, chans), bf16),
            pltpu.VMEM((area, n * area // 2), bf16),
            pltpu.VMEM((3 * chans, area), f32),
            plane, plane, pltpu.VMEM((2, frames, cols * rows, chans), f32),
            pltpu.VMEM((n, stat, chans), f32),
            pltpu.VMEM((stat, chans), f32),
            pltpu.VMEM((n, 2 * frames, chans), f32),
            pltpu.VMEM((n, 2 * frames, chans), f32),
            pltpu.VMEM((n, lat, area // 2), f32),
            pltpu.VMEM((n, lat, area // 2), f32),
            dma((2, 3, 3)), dma((5,)), dma((3, 8)), dma((3, 8)), dma((8,)), dma((8,)),
            dma((3, n)), dma((3, n)), dma((1, n)), dma((1, n)),
        ],
        compiler_params=pltpu.CompilerParams(
            collective_id=0, has_side_effects=True, vmem_limit_bytes=56 * 1024 * 1024
        ),
        cost_estimate=pl.CostEstimate(
            flops=4 * area * 27 * chans * chans, bytes_accessed=4 * 27 * chans * chans, transcendentals=2 * area * chans
        ),
    )(
        second_gain, second_shift, first_gain, first_shift, latent_kernel,
        output_grad, second_input, first_input,
        second_kernel.reshape(9, 3, chans, chans), first_kernel.reshape(9, 3, chans, chans),
        jnp.asarray(group), jnp.asarray(place),
    )
    return out.reshape(4 * lat, tokens)


def solution(mesh):
    cells = P("tm", None, "tile", None)
    return jax.shard_map(
        functools.partial(shards, mesh.shape["tm"], mesh.shape["tile"]),
        mesh=mesh,
        in_specs=(cells,) * 3 + (P(),) * 7,
        out_specs=P(None, ("tm", "tile")),
        check_vma=False,
    )
```

```python
import functools

import jax
import jax.numpy as jnp
import ml_dtypes
import numpy as np
from jax import lax
from jax.experimental import pallas as pl
from jax.experimental.pallas import tpu as pltpu
from jax.sharding import PartitionSpec as P

GROUPS = 32
MESH = pl.DeviceIdType.MESH
epsilon = 1e-05
NT = (((1,), (1,)), ((), ()))


def split3(value):
    hi = value.astype(jnp.bfloat16).astype(jnp.float32)
    rest = value - hi
    mid = rest.astype(jnp.bfloat16).astype(jnp.float32)
    return hi, mid, rest - mid


def times_exact(value, ones):
    rows = value.shape[0]
    parts = jnp.concatenate(split3(value), axis=0).astype(jnp.bfloat16)
    out = jnp.dot(parts, ones, preferred_element_type=jnp.float32)
    return out[:rows] + out[rows : 2 * rows] + out[2 * rows :]


def body(
    n_tm, n,
    gain2, shift2, gain1, shift1, lat_ref,
    g_hbm, x2_hbm, x1_hbm, k2_hbm, k1_hbm, group_hbm, place_hbm,
    out_ref,
    raw, x_s, x_b, x_e, q_e, x_f, q_b, q_f, norm_out, norm_in, g1, g2, g3, kb2, kb1, group_m, place_m, acc, xhat_s, coef_s, q_s,
    mom, mom_all, sums2, sums1, outgoing, incoming,
    k_sem, c_sem, halo_send, halo_recv, e_send, e_recv, st_send, st_recv, a_send, a_recv,
):
    tm = lax.axis_index("tm")
    me = lax.axis_index("tile")
    frames, rows, cols, chans = g_hbm.shape
    lat = lat_ref.shape[1]
    spot = cols * rows
    area = frames * spot
    cells = float(rows * cols * n * (chans // GROUPS))
    has_l, has_r = me > 0, me < n - 1
    has_p, has_f = tm > 0, tm < n_tm - 1
    f32 = jnp.float32

    def load(src, dst, which, a, c):
        return pltpu.make_async_copy(
            src.at[pl.ds(3 * a, 3), c],
            dst.at[pl.ds(3 * a, 3), :, pl.ds(c * chans, chans)],
            k_sem.at[which, a, c],
        )

    const_loads = [
        pltpu.make_async_copy(group_hbm, group_m, c_sem.at[0]),
        pltpu.make_async_copy(place_hbm, place_m, c_sem.at[1]),
    ]
    inputs = [
        pltpu.make_async_copy(src, raw.at[i], c_sem.at[2 + i])
        for i, src in enumerate((g_hbm, x2_hbm, x1_hbm))
    ]
    for copy in inputs:
        copy.start()
    const_loads[0].start()
    for c in range(3):
        load(k2_hbm, kb2, 0, 2, c).start()

    for buf in (g1, g2, g3):
        @pl.when(jnp.logical_not(has_l))
        def _():
            buf[:, 0] = jnp.zeros((frames + 2, rows, chans), jnp.bfloat16)

        @pl.when(jnp.logical_not(has_r))
        def _():
            buf[:, cols + 1] = jnp.zeros((frames + 2, rows, chans), jnp.bfloat16)

        @pl.when(jnp.logical_not(has_f))
        def _():
            buf[pl.ds(frames, 2)] = jnp.zeros((2, cols + 2, rows, chans), jnp.bfloat16)

    barrier = pltpu.get_barrier_semaphore()
    for d in range(1, n):
        pl.semaphore_signal(
            barrier, inc=1, device_id={"tm": tm, "tile": lax.rem(me + d, n)}, device_id_type=MESH
        )
    for dt, ok in ((-1, has_p), (1, has_f)):
        @pl.when(ok)
        def _():
            pl.semaphore_signal(
                barrier, inc=1, device_id={"tm": tm + dt, "tile": me}, device_id_type=MESH
            )

    def as_int(flag):
        return jnp.where(flag, 1, 0).astype(jnp.int32)

    peers = (n - 1) + as_int(has_p) + as_int(has_f)

    to_w = lax.broadcasted_iota(jnp.int32, (cols, rows, spot), 0)
    to_h = lax.broadcasted_iota(jnp.int32, (cols, rows, spot), 1)
    source = lax.broadcasted_iota(jnp.int32, (cols, rows, spot), 2)
    turn = jnp.where(source == to_h * cols + to_w, 1.0, 0.0).reshape(spot, spot).astype(jnp.bfloat16)

    def turned(i, f):
        return jnp.dot(turn, raw[i, f].reshape(spot, chans), preferred_element_type=f32)

    inputs[0].wait()
    for f in range(frames):
        g1[f, 1 : 1 + cols] = turned(0, f).astype(jnp.bfloat16).reshape(cols, rows, chans)
    for k in range(2):
        inputs[1 + k].wait()
        for f in range(frames):
            x = turned(1 + k, f)
            x_s[k, f] = x
            x_b[k, f] = x.astype(jnp.bfloat16).reshape(cols, rows, chans)
            at = 2 * frames * k + 2 * f
            mom[me, pl.ds(at, 1)] = jnp.sum(x, axis=0, keepdims=True)
            mom[me, pl.ds(at + 1, 1)] = jnp.sum(x * x, axis=0, keepdims=True)
    pl.semaphore_wait(barrier, peers)

    def halo(buf, stage):
        def copy(src, dst, slot, dt, dw):
            return pltpu.make_async_remote_copy(
                src_ref=src, dst_ref=dst,
                send_sem=halo_send.at[stage, slot], recv_sem=halo_recv.at[stage, slot],
                device_id={"tm": tm + dt, "tile": me + dw}, device_id_type=MESH,
            )

        own, next_two, first_two = pl.ds(0, frames), pl.ds(frames, 2), pl.ds(0, 2)
        inner = pl.ds(2, cols - 2)
        both = jnp.logical_and
        side = [
            (copy(buf.at[own, cols], buf.at[own, 0], 0, 0, 1), has_r, has_l),
            (copy(buf.at[own, 1], buf.at[own, cols + 1], 1, 0, -1), has_l, has_r),
        ]
        edges = [
            (copy(buf.at[first_two, col], buf.at[next_two, col], slot, -1, 0), has_p, has_f)
            for slot, col in ((2, 1), (3, cols))
        ]
        inners = [
            [(copy(buf.at[f, inner], buf.at[frames + f, inner], 4 + f, -1, 0), has_p, has_f)]
            for f in range(2)
        ]
        passed = [
            (copy(buf.at[next_two, cols], buf.at[next_two, 0], 6, 0, 1),
             both(has_f, has_r), both(has_f, has_l)),
            (copy(buf.at[next_two, 1], buf.at[next_two, cols + 1], 7, 0, -1),
             both(has_f, has_l), both(has_f, has_r)),
        ]
        if stage:
            return [], [], [[], []], passed
        return side, edges, inners, passed

    def edge_moves(src_last, src_first, dst, at):
        def copy(src, to, slot, dw):
            return pltpu.make_async_remote_copy(
                src_ref=src, dst_ref=to, send_sem=e_send.at[slot], recv_sem=e_recv.at[slot],
                device_id={"tm": tm, "tile": me + dw}, device_id_type=MESH,
            )

        return [
            (copy(src_last, dst.at[0], at, 1), has_r, has_l),
            (copy(src_first, dst.at[1], at + 1, -1), has_l, has_r),
        ]

    def next_move(src, dst, k, slot):
        move = pltpu.make_async_remote_copy(
            src_ref=src, dst_ref=dst,
            send_sem=halo_send.at[k + 1, slot], recv_sem=halo_recv.at[k + 1, slot],
            device_id={"tm": tm - 1, "tile": me}, device_id_type=MESH,
        )
        return (move, has_p, has_f)

    x_next = [[next_move(x_b.at[k, pl.ds(0, 2)], x_f.at[k], k, 5)] for k in range(2)]
    q_next = [[next_move(q_b.at[k, f], q_f.at[k, f], k, 2 + f) for f in range(2)] for k in range(2)]
    norm_next = [[next_move(norm_out.at[k], norm_in.at[k], k, 4)] for k in range(2)]

    every = pl.ds(0, frames)
    x_edges = [
        edge_moves(x_b.at[k, every, cols - 1], x_b.at[k, every, 0], x_e.at[k], 2 * k) for k in range(2)
    ]
    q_edges = [
        edge_moves(
            q_s.at[k, every, pl.ds(spot - rows, rows)], q_s.at[k, every, pl.ds(0, rows)], q_e.at[k], 4 + 2 * k
        )
        for k in range(2)
    ]

    def start(moves):
        for move, sends, _ in moves:
            pl.when(sends)(move.start)

    def arrive(moves):
        for move, _, receives in moves:
            pl.when(receives)(move.wait_recv)

    def sent(moves):
        for move, sends, _ in moves:
            pl.when(sends)(move.wait_send)

    def spread(buf, sends, recvs, index, source=None):
        out = []
        for d in range(1, n):
            to = lax.rem(me + d, n)
            src = buf.at[me] if source is None else source.at[to]
            out.append((
                pltpu.make_async_remote_copy(
                    src_ref=src, dst_ref=buf.at[me],
                    send_sem=sends.at[index, d], recv_sem=recvs.at[index, d],
                    device_id={"tm": tm, "tile": to}, device_id_type=MESH,
                ),
                pltpu.make_async_remote_copy(
                    src_ref=src, dst_ref=buf.at[lax.rem(me - d + n, n)],
                    send_sem=sends.at[index, d], recv_sem=recvs.at[index, d],
                    device_id={"tm": tm, "tile": to}, device_id_type=MESH,
                ),
            ))
        return out

    def total(buf):
        out = buf[0]
        for s in range(1, n):
            out = out + buf[s]
        return out

    halos = [halo(buf, i) for i, buf in enumerate((g1, g2, g3))]

    mom_moves = spread(mom, st_send, st_recv, 0)
    start(halos[0][0])
    for move, _ in mom_moves:
        move.start()
    start(halos[0][1])
    for part in halos[0][2]:
        start(part)
    for a in (1, 0):
        for c in range(3):
            load(k2_hbm, kb2, 0, a, c).start()
    for k in range(2):
        start(x_edges[k])
        start(x_next[k])

    lane_h = lax.rem(lax.broadcasted_iota(jnp.int32, (chans, spot), 1), rows)
    not_last, not_first = lane_h < rows - 1, lane_h > 0

    first_groups = [[(2, 1)], [(2, 0), (2, 2)], [(1, 1)], [(1, 0), (1, 2)], [(0, 1), (0, 0), (0, 2)]]
    later_groups = [[(2, 1)], [(2, 0), (2, 2)], [(1, 1), (0, 1)], [(1, 0), (1, 2), (0, 0), (0, 2)]]

    def group_ready(moves, step, form, between=lambda: None):
        side, edges, inners, passed = moves
        if step == 1:
            arrive(side)
        elif step == 2:
            arrive(edges)
            form()
            start(passed)
            between()
            arrive(inners[0])
        elif step == 3:
            arrive(passed)
        elif step == 4:
            arrive(inners[1])

    def pixels_of(buf, pairs):
        return jnp.concatenate(
            [buf[2 - a : 2 - a + frames, 2 - c : 2 - c + cols].reshape(area, chans) for a, c in pairs], axis=1
        )

    def conv(buf, kb, k_hbm, which, moves, form, between):
        for step, pairs in enumerate(later_groups if which else first_groups):
            group_ready(moves, step, form, between)
            for a, c in pairs:
                load(k_hbm, kb, which, a, c).wait()
            weights = jnp.concatenate(
                [kb[3 * a : 3 * a + 3, :, c * chans : (c + 1) * chans].reshape(3 * chans, chans) for a, c in pairs],
                axis=1,
            )
            part = lax.dot_general(weights, pixels_of(buf, pairs), NT, preferred_element_type=f32)
            acc[...] = part if step == 0 else acc[...] + part

    def section(k, gain, shift, buf, nxt, kb, k_hbm, moves, form, sums, index):
        inv, averages = [], []

        def factors():
            if k == 0:
                for _, move in mom_moves:
                    move.wait_recv()
                for a in (2, 1, 0):
                    for c in range(3):
                        load(k1_hbm, kb1, 1, a, c).start()
                const_loads[1].start()
                const_loads[0].wait()
                mom_all[...] = times_exact(total(mom), group_m[...])
            for f in range(frames):
                at = 2 * frames * k + 2 * f
                mean = mom_all[at : at + 1] / cells
                var = mom_all[at + 1 : at + 2] / cells - mean * mean
                r = lax.rsqrt(var + epsilon)
                inv.append(r)
                averages.append(mean)
                xhat = (x_s[k, f] - mean) * r
                z = xhat * gain + shift
                sig = jax.nn.sigmoid(z)
                xhat_s[f] = xhat
                coef_s[f] = sig * (1.0 + z * (1.0 - sig)) * gain

        conv(buf, kb, k_hbm, k, moves, form, factors)
        for f in range(frames):
            at = pl.ds(f * spot, spot)
            up = jnp.where(not_last, pltpu.roll(acc[:chans, at], spot - 1, 1), 0.0)
            down = jnp.where(not_first, pltpu.roll(acc[2 * chans :, at], 1, 1), 0.0)
            q = (up + acc[chans : 2 * chans, at] + down).T * coef_s[f]
            q_s[k, f] = q
            if f < 2:
                q_b[k, f] = q.astype(jnp.bfloat16).reshape(cols, rows, chans)
            sums[me, pl.ds(2 * f, 1)] = jnp.sum(q, axis=0, keepdims=True)
            sums[me, pl.ds(2 * f + 1, 1)] = jnp.sum(q * xhat_s[f], axis=0, keepdims=True)
        sum_moves = spread(sums, st_send, st_recv, index)
        for move, _ in sum_moves:
            move.start()
        start(q_edges[k])
        start(q_next[k])
        for _, move in sum_moves:
            move.wait_recv()
        means = times_exact(total(sums), group_m[...]) / cells
        for f in range(2):
            for i, row in enumerate((averages[f], inv[f], means[2 * f : 2 * f + 1], means[2 * f + 1 : 2 * f + 2])):
                norm_out[k, pl.ds(4 * f + i, 1)] = row
        start(norm_next[k])
        for f in range(frames):
            m1, m2 = means[2 * f : 2 * f + 1], means[2 * f + 1 : 2 * f + 2]
            own = buf[f, 1 : 1 + cols].reshape(spot, chans).astype(f32)
            dx = own + inv[f] * (q_s[k, f] - m1 - xhat_s[f] * m2)
            nxt[f, 1 : 1 + cols] = dx.astype(jnp.bfloat16).reshape(cols, rows, chans)
        arrive(x_edges[k])
        arrive(q_edges[k])
        for at, (col, there) in enumerate(((0, has_l), (cols + 1, has_r))):
            @pl.when(there)
            def _():
                for f in range(frames):
                    m1, m2 = means[2 * f : 2 * f + 1], means[2 * f + 1 : 2 * f + 2]
                    xhat = (x_e[k, at, f].astype(f32) - averages[f]) * inv[f]
                    dx = buf[f, col].astype(f32) + inv[f] * (q_e[k, at, f] - m1 - xhat * m2)
                    nxt[f, col] = dx.astype(jnp.bfloat16)

        def form_next():
            arrive(x_next[k])
            arrive(q_next[k])
            arrive(norm_next[k])

            @pl.when(has_f)
            def _():
                for f in range(2):
                    mean, r, m1, m2 = (norm_in[k, 4 * f + i : 4 * f + i + 1] for i in range(4))
                    xhat = (x_f[k, f].reshape(spot, chans).astype(f32) - mean) * r
                    g = buf[frames + f, 1 : 1 + cols].reshape(spot, chans).astype(f32)
                    dx = g + r * (q_f[k, f].reshape(spot, chans).astype(f32) - m1 - xhat * m2)
                    nxt[frames + f, 1 : 1 + cols] = dx.astype(jnp.bfloat16).reshape(cols, rows, chans)

        return sum_moves, form_next

    def as_row(ref):
        return ref[...].reshape(1, chans)

    moves2, form2 = section(
        0, as_row(gain2), as_row(shift2), g1, g2, kb2, k2_hbm, halos[0], lambda: None, sums2, 1
    )
    moves1, form1 = section(1, as_row(gain1), as_row(shift1), g2, g3, kb1, k1_hbm, halos[1], form2, sums1, 2)

    result = None
    for step, pairs in enumerate(later_groups):
        group_ready(halos[2], step, form1)
        weights = jnp.concatenate(
            [jnp.concatenate([lat_ref[9 * a + 3 * b + c] for a, c in pairs], axis=1) for b in range(3)], axis=0
        )
        part = lax.dot_general(weights, pixels_of(g3, pairs), NT, preferred_element_type=f32)
        result = part if result is None else result + part
    lane = lax.broadcasted_iota(jnp.int32, (lat, area), 1)
    lane_row = lax.rem(lane, rows)
    up = jnp.where(lane_row < rows - 1, pltpu.roll(result[:lat], area - 1, 1), 0.0)
    down = jnp.where(lane_row > 0, pltpu.roll(result[2 * lat :], 1, 1), 0.0)
    pixel = up + result[lat : 2 * lat] + down
    const_loads[1].wait()
    placed = times_exact(pixel, place_m[...])
    half = area // 2
    for j in range(n):
        outgoing[j] = placed[:, j * half : (j + 1) * half]
    last = spread(incoming, a_send, a_recv, 0, outgoing)
    for move, _ in last:
        move.start()
    incoming[me] = outgoing[me]
    for _, move in last:
        move.wait_recv()
    width = n * cols // 2
    low = lax.rem(lax.broadcasted_iota(jnp.int32, (lat, half), 1), width) < width // 2
    lower = upper = jnp.zeros((lat, half), f32)
    for s in range(n):
        got = incoming[s]
        lower = lower + pltpu.roll(jnp.where(low, got, 0.0), s * (cols // 2), 1)
        upper = upper + pltpu.roll(jnp.where(low, 0.0, got), (half + s * (cols // 2) - width // 2) % half, 1)
    out_ref[...] = jnp.concatenate([lower, upper], axis=1)

    for side, edges, inners, passed in halos:
        for part in (side, edges, inners[0], inners[1], passed):
            sent(part)
    for moves in (*x_edges, *q_edges, *x_next, *q_next, *norm_next):
        sent(moves)
    for moves in (mom_moves, moves2, moves1, last):
        for move, _ in moves:
            move.wait_send()


def shards(
    n_tm, n,
    first_input, second_input, output_grad,
    first_gain, first_shift, first_kernel,
    second_gain, second_shift, second_kernel,
    latent_kernel,
):
    frames, rows, cols, chans = first_input.shape
    lat = latent_kernel.shape[1]
    area = frames * rows * cols
    group_of = np.arange(chans) // (chans // GROUPS)
    group = (group_of[:, None] == group_of[None]).astype(ml_dtypes.bfloat16)
    per = frames * (rows // 2) // n
    tokens = area // 4
    f, w, h = np.meshgrid(np.arange(frames), np.arange(cols), np.arange(rows), indexing="ij")
    line = f * (rows // 2) + h // 2
    width = n * cols // 2
    target = (line // per) * (area // 2) + (h % 2) * (width // 2) + (w % 2) * tokens + (line % per) * width + w // 2
    place = (target.reshape(-1, 1) == np.arange(n * area // 2)[None]).astype(ml_dtypes.bfloat16)

    bf16, f32 = jnp.bfloat16, jnp.float32
    vmem = pl.BlockSpec(memory_space=pltpu.VMEM)
    anywhere = pl.BlockSpec(memory_space=pl.ANY)
    grid_buf = pltpu.VMEM((frames + 2, cols + 2, rows, chans), bf16)
    kernel_buf = pltpu.VMEM((9, chans, 3 * chans), bf16)
    plane = pltpu.VMEM((frames, cols * rows, chans), f32)
    next_buf = pltpu.VMEM((2, 2, cols, rows, chans), bf16)
    stat = -(-4 * frames // 8) * 8
    dma = pltpu.SemaphoreType.DMA
    out = pl.pallas_call(
        functools.partial(body, n_tm, n),
        out_shape=jax.ShapeDtypeStruct((lat, area), f32),
        in_specs=[vmem] * 5 + [anywhere] * 7,
        out_specs=vmem,
        scratch_shapes=[
            pltpu.VMEM((3, frames, rows, cols, chans), bf16),
            pltpu.VMEM((2, frames, rows * cols, chans), f32),
            pltpu.VMEM((2, frames, cols, rows, chans), bf16),
            pltpu.VMEM((2, 2, frames, rows, chans), bf16),
            pltpu.VMEM((2, 2, frames, rows, chans), f32),
            next_buf, next_buf, next_buf,
            pltpu.VMEM((2, 8, chans), f32),
            pltpu.VMEM((2, 8, chans), f32),
            grid_buf, grid_buf, grid_buf, kernel_buf, kernel_buf,
            pltpu.VMEM((chans, chans), bf16),
            pltpu.VMEM((area, n * area // 2), bf16),
            pltpu.VMEM((3 * chans, area), f32),
            plane, plane, pltpu.VMEM((2, frames, cols * rows, chans), f32),
            pltpu.VMEM((n, stat, chans), f32),
            pltpu.VMEM((stat, chans), f32),
            pltpu.VMEM((n, 2 * frames, chans), f32),
            pltpu.VMEM((n, 2 * frames, chans), f32),
            pltpu.VMEM((n, lat, area // 2), f32),
            pltpu.VMEM((n, lat, area // 2), f32),
            dma((2, 3, 3)), dma((5,)), dma((3, 8)), dma((3, 8)), dma((8,)), dma((8,)),
            dma((3, n)), dma((3, n)), dma((1, n)), dma((1, n)),
        ],
        compiler_params=pltpu.CompilerParams(
            collective_id=0, has_side_effects=True, vmem_limit_bytes=56 * 1024 * 1024
        ),
        cost_estimate=pl.CostEstimate(
            flops=4 * area * 27 * chans * chans, bytes_accessed=4 * 27 * chans * chans, transcendentals=2 * area * chans
        ),
    )(
        second_gain, second_shift, first_gain, first_shift, latent_kernel,
        output_grad, second_input, first_input,
        second_kernel.reshape(9, 3, chans, chans), first_kernel.reshape(9, 3, chans, chans),
        jnp.asarray(group), jnp.asarray(place),
    )
    return out.reshape(4 * lat, tokens)


def solution(mesh):
    cells = P("tm", None, "tile", None)
    return jax.shard_map(
        functools.partial(shards, mesh.shape["tm"], mesh.shape["tile"]),
        mesh=mesh,
        in_specs=(cells,) * 3 + (P(),) * 7,
        out_specs=P(None, ("tm", "tile")),
        check_vma=False,
    )
```

```python
import functools

import jax
import jax.numpy as jnp
import ml_dtypes
import numpy as np
from jax import lax
from jax.experimental import pallas as pl
from jax.experimental.pallas import tpu as pltpu
from jax.sharding import PartitionSpec as P

GROUPS = 32
MESH = pl.DeviceIdType.MESH
epsilon = 1e-05
NT = (((1,), (1,)), ((), ()))


def split3(value):
    hi = value.astype(jnp.bfloat16).astype(jnp.float32)
    rest = value - hi
    mid = rest.astype(jnp.bfloat16).astype(jnp.float32)
    return hi, mid, rest - mid


def times_exact(value, ones):
    rows = value.shape[0]
    parts = jnp.concatenate(split3(value), axis=0).astype(jnp.bfloat16)
    out = jnp.dot(parts, ones, preferred_element_type=jnp.float32)
    return out[:rows] + out[rows : 2 * rows] + out[2 * rows :]


def body(
    n_tm, n,
    gain2, shift2, gain1, shift1, lat_ref,
    g_hbm, x2_hbm, x1_hbm, k2_hbm, k1_hbm, group_hbm, place_hbm,
    out_ref,
    raw, x_s, x_b, x_e, q_e, x_f, q_b, q_f, norm_out, norm_in, g1, g2, g3, kb2, kb1, group_m, place_m, acc, xhat_s, coef_s, q_s,
    mom, mom_all, sums2, sums1, outgoing, incoming,
    k_sem, c_sem, halo_send, halo_recv, e_send, e_recv, st_send, st_recv, a_send, a_recv,
):
    tm = lax.axis_index("tm")
    me = lax.axis_index("tile")
    frames, rows, cols, chans = g_hbm.shape
    lat = lat_ref.shape[1]
    spot = cols * rows
    area = frames * spot
    cells = float(rows * cols * n * (chans // GROUPS))
    has_l, has_r = me > 0, me < n - 1
    has_p, has_f = tm > 0, tm < n_tm - 1
    f32 = jnp.float32

    def load(src, dst, which, a, c):
        return pltpu.make_async_copy(
            src.at[pl.ds(3 * a, 3), c],
            dst.at[pl.ds(3 * a, 3), :, pl.ds(c * chans, chans)],
            k_sem.at[which, a, c],
        )

    const_loads = [
        pltpu.make_async_copy(group_hbm, group_m, c_sem.at[0]),
        pltpu.make_async_copy(place_hbm, place_m, c_sem.at[1]),
    ]
    inputs = [
        pltpu.make_async_copy(src, raw.at[i], c_sem.at[2 + i])
        for i, src in enumerate((g_hbm, x2_hbm, x1_hbm))
    ]
    for copy in inputs:
        copy.start()
    const_loads[0].start()
    for c in range(3):
        load(k2_hbm, kb2, 0, 2, c).start()

    for buf in (g1, g2, g3):
        @pl.when(jnp.logical_not(has_l))
        def _():
            buf[:, 0] = jnp.zeros((frames + 2, rows, chans), jnp.bfloat16)

        @pl.when(jnp.logical_not(has_r))
        def _():
            buf[:, cols + 1] = jnp.zeros((frames + 2, rows, chans), jnp.bfloat16)

        @pl.when(jnp.logical_not(has_f))
        def _():
            buf[pl.ds(frames, 2)] = jnp.zeros((2, cols + 2, rows, chans), jnp.bfloat16)

    barrier = pltpu.get_barrier_semaphore()
    for d in range(1, n):
        pl.semaphore_signal(
            barrier, inc=1, device_id={"tm": tm, "tile": lax.rem(me + d, n)}, device_id_type=MESH
        )
    for dt, ok in ((-1, has_p), (1, has_f)):
        @pl.when(ok)
        def _():
            pl.semaphore_signal(
                barrier, inc=1, device_id={"tm": tm + dt, "tile": me}, device_id_type=MESH
            )

    def as_int(flag):
        return jnp.where(flag, 1, 0).astype(jnp.int32)

    peers = (n - 1) + as_int(has_p) + as_int(has_f)

    to_w = lax.broadcasted_iota(jnp.int32, (cols, rows, spot), 0)
    to_h = lax.broadcasted_iota(jnp.int32, (cols, rows, spot), 1)
    source = lax.broadcasted_iota(jnp.int32, (cols, rows, spot), 2)
    turn = jnp.where(source == to_h * cols + to_w, 1.0, 0.0).reshape(spot, spot).astype(jnp.bfloat16)

    def turned(i, f):
        return jnp.dot(turn, raw[i, f].reshape(spot, chans), preferred_element_type=f32)

    inputs[0].wait()
    for f in range(frames):
        g1[f, 1 : 1 + cols] = turned(0, f).astype(jnp.bfloat16).reshape(cols, rows, chans)
    for k in range(2):
        inputs[1 + k].wait()
        for f in range(frames):
            x = turned(1 + k, f)
            x_s[k, f] = x
            x_b[k, f] = x.astype(jnp.bfloat16).reshape(cols, rows, chans)
            at = 2 * frames * k + 2 * f
            mom[me, pl.ds(at, 1)] = jnp.sum(x, axis=0, keepdims=True)
            mom[me, pl.ds(at + 1, 1)] = jnp.sum(x * x, axis=0, keepdims=True)
    pl.semaphore_wait(barrier, peers)

    def halo(buf, stage):
        def copy(src, dst, slot, dt, dw):
            return pltpu.make_async_remote_copy(
                src_ref=src, dst_ref=dst,
                send_sem=halo_send.at[stage, slot], recv_sem=halo_recv.at[stage, slot],
                device_id={"tm": tm + dt, "tile": me + dw}, device_id_type=MESH,
            )

        own, next_two, first_two = pl.ds(0, frames), pl.ds(frames, 2), pl.ds(0, 2)
        inner = pl.ds(2, cols - 2)
        both = jnp.logical_and
        side = [
            (copy(buf.at[own, cols], buf.at[own, 0], 0, 0, 1), has_r, has_l),
            (copy(buf.at[own, 1], buf.at[own, cols + 1], 1, 0, -1), has_l, has_r),
        ]
        edges = [
            (copy(buf.at[first_two, col], buf.at[next_two, col], slot, -1, 0), has_p, has_f)
            for slot, col in ((2, 1), (3, cols))
        ]
        inners = [
            [(copy(buf.at[f, inner], buf.at[frames + f, inner], 4 + f, -1, 0), has_p, has_f)]
            for f in range(2)
        ]
        passed = [
            (copy(buf.at[next_two, cols], buf.at[next_two, 0], 6, 0, 1),
             both(has_f, has_r), both(has_f, has_l)),
            (copy(buf.at[next_two, 1], buf.at[next_two, cols + 1], 7, 0, -1),
             both(has_f, has_l), both(has_f, has_r)),
        ]
        if stage:
            return [], [], [[], []], passed
        return side, edges, inners, passed

    def edge_moves(src_last, src_first, dst, at):
        def copy(src, to, slot, dw):
            return pltpu.make_async_remote_copy(
                src_ref=src, dst_ref=to, send_sem=e_send.at[slot], recv_sem=e_recv.at[slot],
                device_id={"tm": tm, "tile": me + dw}, device_id_type=MESH,
            )

        return [
            (copy(src_last, dst.at[0], at, 1), has_r, has_l),
            (copy(src_first, dst.at[1], at + 1, -1), has_l, has_r),
        ]

    def next_move(src, dst, k, slot):
        move = pltpu.make_async_remote_copy(
            src_ref=src, dst_ref=dst,
            send_sem=halo_send.at[k + 1, slot], recv_sem=halo_recv.at[k + 1, slot],
            device_id={"tm": tm - 1, "tile": me}, device_id_type=MESH,
        )
        return (move, has_p, has_f)

    x_next = [[next_move(x_b.at[k, pl.ds(0, 2)], x_f.at[k], k, 5)] for k in range(2)]
    q_next = [[next_move(q_b.at[k, f], q_f.at[k, f], k, 2 + f) for f in range(2)] for k in range(2)]
    norm_next = [[next_move(norm_out.at[k], norm_in.at[k], k, 4)] for k in range(2)]

    every = pl.ds(0, frames)
    x_edges = [
        edge_moves(x_b.at[k, every, cols - 1], x_b.at[k, every, 0], x_e.at[k], 2 * k) for k in range(2)
    ]
    q_edges = [
        edge_moves(
            q_s.at[k, every, pl.ds(spot - rows, rows)], q_s.at[k, every, pl.ds(0, rows)], q_e.at[k], 4 + 2 * k
        )
        for k in range(2)
    ]

    def start(moves):
        for move, sends, _ in moves:
            pl.when(sends)(move.start)

    def arrive(moves):
        for move, _, receives in moves:
            pl.when(receives)(move.wait_recv)

    def sent(moves):
        for move, sends, _ in moves:
            pl.when(sends)(move.wait_send)

    def spread(buf, sends, recvs, index, source=None):
        out = []
        for d in range(1, n):
            to = lax.rem(me + d, n)
            src = buf.at[me] if source is None else source.at[to]
            out.append((
                pltpu.make_async_remote_copy(
                    src_ref=src, dst_ref=buf.at[me],
                    send_sem=sends.at[index, d], recv_sem=recvs.at[index, d],
                    device_id={"tm": tm, "tile": to}, device_id_type=MESH,
                ),
                pltpu.make_async_remote_copy(
                    src_ref=src, dst_ref=buf.at[lax.rem(me - d + n, n)],
                    send_sem=sends.at[index, d], recv_sem=recvs.at[index, d],
                    device_id={"tm": tm, "tile": to}, device_id_type=MESH,
                ),
            ))
        return out

    def total(buf):
        out = buf[0]
        for s in range(1, n):
            out = out + buf[s]
        return out

    halos = [halo(buf, i) for i, buf in enumerate((g1, g2, g3))]

    mom_moves = spread(mom, st_send, st_recv, 0)
    start(halos[0][0])
    for move, _ in mom_moves:
        move.start()
    start(halos[0][1])
    for part in halos[0][2]:
        start(part)
    for a in (1, 0):
        for c in range(3):
            load(k2_hbm, kb2, 0, a, c).start()
    for k in range(2):
        start(x_edges[k])

    lane_h = lax.rem(lax.broadcasted_iota(jnp.int32, (chans, spot), 1), rows)
    not_last, not_first = lane_h < rows - 1, lane_h > 0

    first_groups = [[(2, 1)], [(2, 0), (2, 2)], [(1, 1)], [(1, 0), (1, 2)], [(0, 1), (0, 0), (0, 2)]]
    later_groups = [[(2, 1)], [(2, 0), (2, 2)], [(1, 1), (0, 1)], [(1, 0), (1, 2), (0, 0), (0, 2)]]

    def group_ready(moves, step, form, between=lambda: None):
        side, edges, inners, passed = moves
        if step == 1:
            arrive(side)
        elif step == 2:
            arrive(edges)
            form()
            start(passed)
            between()
            arrive(inners[0])
        elif step == 3:
            arrive(passed)
        elif step == 4:
            arrive(inners[1])

    def pixels_of(buf, pairs):
        return jnp.concatenate(
            [buf[2 - a : 2 - a + frames, 2 - c : 2 - c + cols].reshape(area, chans) for a, c in pairs], axis=1
        )

    def conv(buf, kb, k_hbm, which, moves, form, between):
        for step, pairs in enumerate(later_groups if which else first_groups):
            group_ready(moves, step, form, between)
            for a, c in pairs:
                load(k_hbm, kb, which, a, c).wait()
            weights = jnp.concatenate(
                [kb[3 * a : 3 * a + 3, :, c * chans : (c + 1) * chans].reshape(3 * chans, chans) for a, c in pairs],
                axis=1,
            )
            part = lax.dot_general(weights, pixels_of(buf, pairs), NT, preferred_element_type=f32)
            acc[...] = part if step == 0 else acc[...] + part

    def section(k, gain, shift, buf, nxt, kb, k_hbm, moves, form, sums, index):
        inv, averages = [], []

        def factors():
            if k == 0:
                for _, move in mom_moves:
                    move.wait_recv()
                for a in (2, 1, 0):
                    for c in range(3):
                        load(k1_hbm, kb1, 1, a, c).start()
                const_loads[1].start()
                const_loads[0].wait()
                mom_all[...] = times_exact(total(mom), group_m[...])
            else:
                start(x_next[1])
            for f in range(frames):
                at = 2 * frames * k + 2 * f
                mean = mom_all[at : at + 1] / cells
                var = mom_all[at + 1 : at + 2] / cells - mean * mean
                r = lax.rsqrt(var + epsilon)
                inv.append(r)
                averages.append(mean)
                xhat = (x_s[k, f] - mean) * r
                z = xhat * gain + shift
                sig = jax.nn.sigmoid(z)
                xhat_s[f] = xhat
                coef_s[f] = sig * (1.0 + z * (1.0 - sig)) * gain

        conv(buf, kb, k_hbm, k, moves, form, factors)
        if k == 0:
            start(x_next[0])
        for f in range(frames):
            at = pl.ds(f * spot, spot)
            up = jnp.where(not_last, pltpu.roll(acc[:chans, at], spot - 1, 1), 0.0)
            down = jnp.where(not_first, pltpu.roll(acc[2 * chans :, at], 1, 1), 0.0)
            q = (up + acc[chans : 2 * chans, at] + down).T * coef_s[f]
            q_s[k, f] = q
            if f < 2:
                q_b[k, f] = q.astype(jnp.bfloat16).reshape(cols, rows, chans)
            sums[me, pl.ds(2 * f, 1)] = jnp.sum(q, axis=0, keepdims=True)
            sums[me, pl.ds(2 * f + 1, 1)] = jnp.sum(q * xhat_s[f], axis=0, keepdims=True)
        sum_moves = spread(sums, st_send, st_recv, index)
        for move, _ in sum_moves:
            move.start()
        start(q_edges[k])
        start(q_next[k])
        for _, move in sum_moves:
            move.wait_recv()
        means = times_exact(total(sums), group_m[...]) / cells
        for f in range(2):
            for i, row in enumerate((averages[f], inv[f], means[2 * f : 2 * f + 1], means[2 * f + 1 : 2 * f + 2])):
                norm_out[k, pl.ds(4 * f + i, 1)] = row
        start(norm_next[k])
        for f in range(frames):
            m1, m2 = means[2 * f : 2 * f + 1], means[2 * f + 1 : 2 * f + 2]
            own = buf[f, 1 : 1 + cols].reshape(spot, chans).astype(f32)
            dx = own + inv[f] * (q_s[k, f] - m1 - xhat_s[f] * m2)
            nxt[f, 1 : 1 + cols] = dx.astype(jnp.bfloat16).reshape(cols, rows, chans)
        arrive(x_edges[k])
        arrive(q_edges[k])
        for at, (col, there) in enumerate(((0, has_l), (cols + 1, has_r))):
            @pl.when(there)
            def _():
                for f in range(frames):
                    m1, m2 = means[2 * f : 2 * f + 1], means[2 * f + 1 : 2 * f + 2]
                    xhat = (x_e[k, at, f].astype(f32) - averages[f]) * inv[f]
                    dx = buf[f, col].astype(f32) + inv[f] * (q_e[k, at, f] - m1 - xhat * m2)
                    nxt[f, col] = dx.astype(jnp.bfloat16)

        def form_next():
            arrive(x_next[k])
            arrive(q_next[k])
            arrive(norm_next[k])

            @pl.when(has_f)
            def _():
                for f in range(2):
                    mean, r, m1, m2 = (norm_in[k, 4 * f + i : 4 * f + i + 1] for i in range(4))
                    xhat = (x_f[k, f].reshape(spot, chans).astype(f32) - mean) * r
                    g = buf[frames + f, 1 : 1 + cols].reshape(spot, chans).astype(f32)
                    dx = g + r * (q_f[k, f].reshape(spot, chans).astype(f32) - m1 - xhat * m2)
                    nxt[frames + f, 1 : 1 + cols] = dx.astype(jnp.bfloat16).reshape(cols, rows, chans)

        return sum_moves, form_next

    def as_row(ref):
        return ref[...].reshape(1, chans)

    moves2, form2 = section(
        0, as_row(gain2), as_row(shift2), g1, g2, kb2, k2_hbm, halos[0], lambda: None, sums2, 1
    )
    moves1, form1 = section(1, as_row(gain1), as_row(shift1), g2, g3, kb1, k1_hbm, halos[1], form2, sums1, 2)

    result = None
    for step, pairs in enumerate(later_groups):
        group_ready(halos[2], step, form1)
        weights = jnp.concatenate(
            [jnp.concatenate([lat_ref[9 * a + 3 * b + c] for a, c in pairs], axis=1) for b in range(3)], axis=0
        )
        part = lax.dot_general(weights, pixels_of(g3, pairs), NT, preferred_element_type=f32)
        result = part if result is None else result + part
    lane = lax.broadcasted_iota(jnp.int32, (lat, area), 1)
    lane_row = lax.rem(lane, rows)
    up = jnp.where(lane_row < rows - 1, pltpu.roll(result[:lat], area - 1, 1), 0.0)
    down = jnp.where(lane_row > 0, pltpu.roll(result[2 * lat :], 1, 1), 0.0)
    pixel = up + result[lat : 2 * lat] + down
    const_loads[1].wait()
    placed = times_exact(pixel, place_m[...])
    half = area // 2
    for j in range(n):
        outgoing[j] = placed[:, j * half : (j + 1) * half]
    last = spread(incoming, a_send, a_recv, 0, outgoing)
    for move, _ in last:
        move.start()
    incoming[me] = outgoing[me]
    for _, move in last:
        move.wait_recv()
    width = n * cols // 2
    low = lax.rem(lax.broadcasted_iota(jnp.int32, (lat, half), 1), width) < width // 2
    lower = upper = jnp.zeros((lat, half), f32)
    for s in range(n):
        got = incoming[s]
        lower = lower + pltpu.roll(jnp.where(low, got, 0.0), s * (cols // 2), 1)
        upper = upper + pltpu.roll(jnp.where(low, 0.0, got), (half + s * (cols // 2) - width // 2) % half, 1)
    out_ref[...] = jnp.concatenate([lower, upper], axis=1)

    for side, edges, inners, passed in halos:
        for part in (side, edges, inners[0], inners[1], passed):
            sent(part)
    for moves in (*x_edges, *q_edges, *x_next, *q_next, *norm_next):
        sent(moves)
    for moves in (mom_moves, moves2, moves1, last):
        for move, _ in moves:
            move.wait_send()


def shards(
    n_tm, n,
    first_input, second_input, output_grad,
    first_gain, first_shift, first_kernel,
    second_gain, second_shift, second_kernel,
    latent_kernel,
):
    frames, rows, cols, chans = first_input.shape
    lat = latent_kernel.shape[1]
    area = frames * rows * cols
    group_of = np.arange(chans) // (chans // GROUPS)
    group = (group_of[:, None] == group_of[None]).astype(ml_dtypes.bfloat16)
    per = frames * (rows // 2) // n
    tokens = area // 4
    f, w, h = np.meshgrid(np.arange(frames), np.arange(cols), np.arange(rows), indexing="ij")
    line = f * (rows // 2) + h // 2
    width = n * cols // 2
    target = (line // per) * (area // 2) + (h % 2) * (width // 2) + (w % 2) * tokens + (line % per) * width + w // 2
    place = (target.reshape(-1, 1) == np.arange(n * area // 2)[None]).astype(ml_dtypes.bfloat16)

    bf16, f32 = jnp.bfloat16, jnp.float32
    vmem = pl.BlockSpec(memory_space=pltpu.VMEM)
    anywhere = pl.BlockSpec(memory_space=pl.ANY)
    grid_buf = pltpu.VMEM((frames + 2, cols + 2, rows, chans), bf16)
    kernel_buf = pltpu.VMEM((9, chans, 3 * chans), bf16)
    plane = pltpu.VMEM((frames, cols * rows, chans), f32)
    next_buf = pltpu.VMEM((2, 2, cols, rows, chans), bf16)
    stat = -(-4 * frames // 8) * 8
    dma = pltpu.SemaphoreType.DMA
    out = pl.pallas_call(
        functools.partial(body, n_tm, n),
        out_shape=jax.ShapeDtypeStruct((lat, area), f32),
        in_specs=[vmem] * 5 + [anywhere] * 7,
        out_specs=vmem,
        scratch_shapes=[
            pltpu.VMEM((3, frames, rows, cols, chans), bf16),
            pltpu.VMEM((2, frames, rows * cols, chans), f32),
            pltpu.VMEM((2, frames, cols, rows, chans), bf16),
            pltpu.VMEM((2, 2, frames, rows, chans), bf16),
            pltpu.VMEM((2, 2, frames, rows, chans), f32),
            next_buf, next_buf, next_buf,
            pltpu.VMEM((2, 8, chans), f32),
            pltpu.VMEM((2, 8, chans), f32),
            grid_buf, grid_buf, grid_buf, kernel_buf, kernel_buf,
            pltpu.VMEM((chans, chans), bf16),
            pltpu.VMEM((area, n * area // 2), bf16),
            pltpu.VMEM((3 * chans, area), f32),
            plane, plane, pltpu.VMEM((2, frames, cols * rows, chans), f32),
            pltpu.VMEM((n, stat, chans), f32),
            pltpu.VMEM((stat, chans), f32),
            pltpu.VMEM((n, 2 * frames, chans), f32),
            pltpu.VMEM((n, 2 * frames, chans), f32),
            pltpu.VMEM((n, lat, area // 2), f32),
            pltpu.VMEM((n, lat, area // 2), f32),
            dma((2, 3, 3)), dma((5,)), dma((3, 8)), dma((3, 8)), dma((8,)), dma((8,)),
            dma((3, n)), dma((3, n)), dma((1, n)), dma((1, n)),
        ],
        compiler_params=pltpu.CompilerParams(
            collective_id=0, has_side_effects=True, vmem_limit_bytes=56 * 1024 * 1024
        ),
        cost_estimate=pl.CostEstimate(
            flops=4 * area * 27 * chans * chans, bytes_accessed=4 * 27 * chans * chans, transcendentals=2 * area * chans
        ),
    )(
        second_gain, second_shift, first_gain, first_shift, latent_kernel,
        output_grad, second_input, first_input,
        second_kernel.reshape(9, 3, chans, chans), first_kernel.reshape(9, 3, chans, chans),
        jnp.asarray(group), jnp.asarray(place),
    )
    return out.reshape(4 * lat, tokens)


def solution(mesh):
    cells = P("tm", None, "tile", None)
    return jax.shard_map(
        functools.partial(shards, mesh.shape["tm"], mesh.shape["tile"]),
        mesh=mesh,
        in_specs=(cells,) * 3 + (P(),) * 7,
        out_specs=P(None, ("tm", "tile")),
        check_vma=False,
    )
```
